32 devices in a mesh: dp: 4 (over y, x), expert: 4 (over z), tensor: 2 (over core).
Axes of the slice: x: 2, y: 2, z: 4, core: 2. Of those that a mesh axis runs over, the one named last changes fastest.
Arguments:
- layer_in: bfloat16 [2048, 2048], P(('dp', 'expert')), may hold values from -6 to 6
- norm_gain: bfloat16 [2048], replicated, may hold values from 0.099609375 to 1.8984375
- query_proj: bfloat16 [2048, 3072], P('dp', 'tensor'), may hold values from -0.125 to 0.125
- latent_proj: bfloat16 [2048, 576], P('dp'), may hold values from -0.125 to 0.125
- latent_gain: bfloat16 [512], replicated, may hold values from 0.099609375 to 1.8984375
- latent_up: bfloat16 [512, 4096], P('dp', 'tensor'), may hold values from -0.25 to 0.25
- output_proj: bfloat16 [2048, 2048], P('tensor', 'dp'), may hold values from -0.75 to 0.75
- ffn_gain: bfloat16 [2048], replicated, may hold values from 0.099609375 to 1.8984375
- router: bfloat16 [2048, 16], replicated, may hold values from -0.0625 to 0.0625
- shared_gate: bfloat16 [2048, 2816], P('dp', 'tensor'), may hold values from -0.125 to 0.125
- shared_up: bfloat16 [2048, 2816], P('dp', 'tensor'), may hold values from -0.125 to 0.125
- shared_down: bfloat16 [2816, 2048], P('tensor', 'dp'), may hold values from -0.109375 to 0.109375
- expert_gate: bfloat16 [16, 2048, 1408], P('expert', None, 'tensor'), may hold values from -0.125 to 0.125
- expert_up: bfloat16 [16, 2048, 1408], P('expert', None, 'tensor'), may hold values from -0.125 to 0.125
- expert_down: bfloat16 [16, 1408, 2048], P('expert', 'tensor'), may hold values from -0.625 to 0.625
- routes: int32 [2048, 6], P(('dp', 'expert')), may hold values from 0 to 15, as said below
- leaf_parent: int32 [8], replicated, may hold values from 0 to 3, as said below
- grad_out: bfloat16 [2048, 2048], P(('dp', 'expert')), may hold values from -6 to 6
Outputs:
- layer_out: bfloat16 [2048, 2048], P(('dp', 'expert'))
- grad_in: float32 [2048, 2048], P(('dp', 'expert'))
- grad_norm_gain: float32 [2048], P(('dp', 'expert'))
- grad_query_proj: float32 [2048, 3072], P(('dp', 'expert'), 'tensor')
- grad_latent_proj: float32 [2048, 576], P(('dp', 'expert'))
- grad_latent_gain: float32 [512], P(('dp', 'expert'))
- grad_latent_up: float32 [512, 4096], P(('dp', 'expert'), 'tensor')
- grad_output_proj: float32 [2048, 2048], P('tensor', ('dp', 'expert'))
- grad_ffn_gain: float32 [2048], P(('dp', 'expert'))
- grad_router: float32 [2048, 16], P(('dp', 'expert'))
- grad_shared_gate: float32 [2048, 2816], P(('dp', 'expert'), 'tensor')
- grad_shared_up: float32 [2048, 2816], P(('dp', 'expert'), 'tensor')
- grad_shared_down: float32 [2816, 2048], P('tensor', ('dp', 'expert'))
- grad_expert_gate: float32 [16, 2048, 1408], P('expert', 'dp', 'tensor')
- grad_expert_up: float32 [16, 2048, 1408], P('expert', 'dp', 'tensor')
- grad_expert_down: float32 [16, 1408, 2048], P('expert', 'tensor', 'dp')
The draws below stay inside these ranges and needn't reach their ends.
Inputs may be any that keep to these rules, and one draw needn't show every extreme that they name: `routes`: A row names 6 different experts. In the rows of each index of dp and expert one expert, the same one for all of them in a draw, is named exactly 96 times, and no other expert more than 96 times. `leaf_parent`: each branch is the parent of exactly 2 leaves.
All inputs are finite; a program needn't handle non-finite values.
Results may differ from the reference program's by a relative error of at most 0.02.
Values may be sent and summed in bfloat16 or wider, within the bound.
No kernel may reach another device: no remote copies, remote signals or barrier semaphores. Data moves between devices by JAX's collectives and lax.ppermute only.
A program may use at most 384 MiB of HBM per device.

```python
import jax
import jax.numpy as jnp
from jax import lax

D = 2048
H = 16
DN = 128
DR = 64
DV = 128
R = 512
FF = 1408
FS = 2816
EXPERTS = 16
TOP = 6
NB = 4
NL = 2
TOK_DEV = 128
TREE = 512
SEG = 32
TRUNK = 128
TOKENS = 2048
CAP = 96
N_EXPERT = 4
N_TENSOR = 2


def draw_routes(key, part):
    block_count = TOKENS // TOK_DEV
    others = EXPERTS - 1
    full_expert = jax.random.randint(jax.random.fold_in(key, 7), (), 0, EXPERTS).astype(jnp.int32)
    row_rank = jnp.arange(TOK_DEV, dtype=jnp.int32)
    column = jnp.arange(TOP, dtype=jnp.int32)

    def one_block(block_index):
        block_key = jax.random.fold_in(key, block_index + 11)
        expert_order = jax.random.permutation(jax.random.fold_in(block_key, 1), others).astype(jnp.int32)
        expert_order = expert_order + (expert_order >= full_expert).astype(jnp.int32)
        row_place = jax.random.permutation(jax.random.fold_in(block_key, 2), TOK_DEV).astype(jnp.int32)
        rotation = jax.random.randint(jax.random.fold_in(block_key, 3), (TOK_DEV,), 0, TOP).astype(jnp.int32)
        is_full = row_rank < CAP
        cycle_start = row_rank * TOP - jnp.minimum(row_rank, CAP)
        full_lead = jnp.where(is_full, 1, 0).astype(jnp.int32)
        cycle_offset = column[None, :] - full_lead[:, None]
        picked = jnp.take(expert_order, (cycle_start[:, None] + cycle_offset) % others)
        row_routes = jnp.where(is_full[:, None] & (column[None, :] == 0), full_expert, picked)
        row_routes = jnp.take_along_axis(row_routes, (column[None, :] + rotation[:, None]) % TOP, axis=1)
        return jnp.zeros((TOK_DEV, TOP), jnp.int32).at[row_place].set(row_routes.astype(jnp.int32))
    return jax.vmap(one_block)(jnp.arange(block_count, dtype=jnp.int32)).reshape(TOKENS, TOP)


def draw_leaf_parent(key, part):
    return (jax.random.permutation(key, NB * NL) // NL).astype(jnp.int32)


def raised(values, rng, source, target, blocks, factor):
    owner, partner = [(jnp.arange(values.shape[axis_at]) // (values.shape[axis_at] // blocks)).reshape([-1 if axis == axis_at else 1 for axis in range(values.ndim)]) for axis_at in (source, target)]
    chosen = jax.random.permutation(rng, blocks)[partner]
    strong = (owner == chosen) | (owner == (partner + blocks // 2) % blocks)
    return jnp.where(strong, factor * values, values)


def block_levels(key, extent, cuts, low, top_value):
    def one(dim, blocks):
        draws = jax.random.uniform(jax.random.fold_in(jax.random.fold_in(key, 6), dim), (blocks,), jnp.float32, low / len(cuts), top_value / len(cuts))
        return jnp.repeat(jnp.exp(draws), extent[dim] // blocks).reshape((-1,) + (1,) * (len(extent) - dim - 1))

    factor_of = one(*cuts[0])
    for cut in cuts[1:]:
        factor_of = factor_of * one(*cut)
    return factor_of


def centred(stream_key, shape, deviation, most, split=(), kind=jnp.bfloat16):
    loudness = block_levels(stream_key, shape, split, -0.22, 0.18) if split else 1.0
    entries = jax.random.normal(stream_key, shape, jnp.float32) * deviation * loudness
    return jnp.minimum(jnp.maximum(entries, -most), most).astype(kind)


def noise_with(stream_key, dims, deviation, bound, cuts, heavy, held_as=jnp.bfloat16):
    array = deviation * jax.random.normal(stream_key, dims, jnp.float32)
    if cuts:
        array = array * block_levels(stream_key, dims, cuts, -0.22, 0.18)
    return jnp.clip(raised(array, jax.random.fold_in(stream_key, 3), *heavy), -bound, bound).astype(held_as)


def setup_inputs(seed: int = 0) -> dict:
    arg_keys = jax.random.split(jax.random.key(seed), 19)
    return {
        "layer_in": noise_with(arg_keys[0], (TOKENS, D), 1.0, 6.0, ((0, 16),), (0, 1, 16, 2.0)),
        "norm_gain": jnp.clip(1.0 + 0.18 * jax.random.normal(arg_keys[1], (D,), jnp.float32), 0.099609375, 1.8984375).astype(jnp.bfloat16),
        "query_proj": centred(arg_keys[2], (D, H * (DN + DR)), D ** -0.5, 0.125, ((0, 4), (1, 2))),
        "latent_proj": centred(arg_keys[3], (D, R + DR), D ** -0.5, 0.125, ((0, 4),)),
        "latent_gain": jnp.clip(1.0 + 0.18 * jax.random.normal(arg_keys[4], (R,), jnp.float32), 0.099609375, 1.8984375).astype(jnp.bfloat16),
        "latent_up": centred(arg_keys[5], (R, H * (DN + DV)), R ** -0.5, 0.25, ((0, 4), (1, 2))),
        "output_proj": centred(arg_keys[6], (H * DV, D), 64 ** -0.5, 0.75, ((0, 2), (1, 4))),
        "ffn_gain": jnp.clip(1.0 + 0.18 * jax.random.normal(arg_keys[7], (D,), jnp.float32), 0.099609375, 1.8984375).astype(jnp.bfloat16),
        "router": centred(arg_keys[8], (D, EXPERTS), (4 * D) ** -0.5, 0.0625),
        "shared_gate": centred(arg_keys[9], (D, FS), D ** -0.5, 0.125, ((0, 4), (1, 2))),
        "shared_up": centred(arg_keys[10], (D, FS), D ** -0.5, 0.125, ((0, 4), (1, 2))),
        "shared_down": centred(arg_keys[11], (FS, D), FS ** -0.5, 0.109375, ((0, 2), (1, 4))),
        "expert_gate": centred(arg_keys[12], (EXPERTS, D, FF), D ** -0.5, 0.125, ((0, 4), (2, 2))),
        "expert_up": centred(arg_keys[13], (EXPERTS, D, FF), D ** -0.5, 0.125, ((0, 4), (2, 2))),
        "expert_down": centred(arg_keys[14], (EXPERTS, FF, D), (FF // 16) ** -0.5, 0.625, ((0, 4), (1, 2))),
        "routes": draw_routes(jax.random.fold_in(arg_keys[18], 71), 0),
        "leaf_parent": draw_leaf_parent(jax.random.fold_in(arg_keys[18], 71), 0),
        "grad_out": noise_with(arg_keys[17], (TOKENS, D), 1.0, 6.0, ((0, 16),), (0, 1, 16, 2.0)),
    }


HIGHEST = lax.Precision.HIGHEST
epsilon = 1e-06
masked_score = -1e+30

@jax.custom_vjp
def low(v):
    return lax.optimization_barrier(v.astype(jnp.bfloat16)).astype(jnp.float32)

@jax.custom_vjp
def low_back(v):
    return v

def low_keep(v):
    return (low(v), None)

def low_pass(kept, grad):
    return (grad,)

def back_keep(v):
    return (v, None)

def back_low(kept, grad):
    return (low(grad),)
low.defvjp(low_keep, low_pass)
low_back.defvjp(back_keep, back_low)

def matmul(left, right):
    return jnp.dot(left, right, precision=HIGHEST, preferred_element_type=jnp.float32)

def rms_norm(values, gain_vector):
    return values * lax.rsqrt(lax.optimization_barrier(jnp.mean(values * values, axis=-1, keepdims=True)) + epsilon) * gain_vector

def rotary_tables(positions, width):
    half_width = width // 2
    freqs = 10000.0 ** (-2.0 * jnp.arange(half_width, dtype=jnp.float32) / width)
    angles = positions.astype(jnp.float32)[:, None] * freqs[None, :]
    return (jnp.cos(angles), jnp.sin(angles))

def rotate(values, cosine, sine):
    half_width = values.shape[-1] // 2
    first_half = values[..., :half_width]
    second_half = values[..., half_width:]
    return jnp.concatenate([first_half * cosine - second_half * sine, second_half * cosine + first_half * sine], axis=-1)

def tree_layout(leaf_parent):
    token_index = jnp.arange(TREE, dtype=jnp.int32)
    beyond = token_index - TRUNK
    in_trunk = token_index < TRUNK
    in_branch = (beyond >= 0) & (beyond < NB * SEG)
    in_leaf = beyond >= NB * SEG
    leaf_offset = beyond - NB * SEG
    leaf_index = jnp.clip(leaf_offset // SEG, 0, NB * NL - 1)
    position = jnp.where(in_trunk, token_index, jnp.where(in_branch, TRUNK + beyond % SEG, TRUNK + SEG + leaf_offset % SEG))
    segment = jnp.where(in_trunk, 0, jnp.where(in_branch, 1 + beyond // SEG, 1 + NB + leaf_index))
    leaf_match = (leaf_index[:, None] == jnp.arange(NB * NL, dtype=jnp.int32)[None, :]).astype(jnp.int32)
    branch_of_leaf = 1 + lax.optimization_barrier(jnp.sum(leaf_match * leaf_parent[None, :], axis=1))
    parent = jnp.where(in_trunk, -1, jnp.where(in_branch, 0, branch_of_leaf))
    grand = jnp.where(in_leaf, 0, -1)
    return (position.astype(jnp.int32), segment.astype(jnp.int32), parent.astype(jnp.int32), grand.astype(jnp.int32))

def visible(query_segment, query_parent, query_grand, query_index, key_segment, key_index):
    same_segment = (query_segment[:, None] == key_segment[None, :]) & (key_index[None, :] <= query_index[:, None])
    ancestor = (key_segment[None, :] == query_parent[:, None]) | (key_segment[None, :] == query_grand[:, None])
    return same_segment | ancestor

def reference(layer_in, norm_gain, query_proj, latent_proj, latent_gain, latent_up, output_proj, ffn_gain, router, shared_gate, shared_up, shared_down, expert_gate, expert_up, expert_down, routes, leaf_parent, grad_out):
    position, segment, parent, grand = tree_layout(leaf_parent)
    cosine, sine = rotary_tables(position, DR)
    token_index = jnp.arange(TREE, dtype=jnp.int32)
    score_scale = (DN + DR) ** (-0.5)
    block_rows = min(512, TREE)
    most_rows = min(TREE, N_EXPERT * CAP)
    slice_width = FF // N_TENSOR
    tree_count = TOKENS // TREE

    def tree_forward(weight_sequence, tree_input, tree_routes):
        first_norm_scale, query_weight, latent_weight, latent_norm_scale, latent_up_weight, output_weight, second_norm_scale, router_weight, shared_gate_weight, shared_up_weight, shared_down_weight, expert_gate_weight, expert_up_weight, expert_down_weight = weight_sequence
        normed = low(rms_norm(tree_input, first_norm_scale))
        query_all = low_back(matmul(normed, query_weight)).reshape(TREE, H, DN + DR)
        query_nope = low(query_all[:, :, :DN])
        query_rope = low(rotate(query_all[:, :, DN:], cosine[:, None, :], sine[:, None, :]))
        latent_all = low_back(matmul(normed, latent_weight))
        latent = low(rms_norm(latent_all[:, :R], latent_norm_scale))
        key_rope = low(rotate(latent_all[:, R:], cosine, sine))
        up_heads = latent_up_weight.reshape(R, H, DN + DV)
        query_latent = low(low_back(jnp.einsum('thd,rhd->thr', query_nope, up_heads[:, :, :DN], precision=HIGHEST)))
        queries = jnp.concatenate([query_latent, query_rope], axis=2)
        keys = jnp.concatenate([latent, key_rope], axis=1)

        def attend(block_index):
            start_row = block_index * block_rows
            block_queries = lax.dynamic_slice_in_dim(queries, start_row, block_rows, 0)
            allowed = visible(lax.dynamic_slice_in_dim(segment, start_row, block_rows, 0), lax.dynamic_slice_in_dim(parent, start_row, block_rows, 0), lax.dynamic_slice_in_dim(grand, start_row, block_rows, 0), lax.dynamic_slice_in_dim(token_index, start_row, block_rows, 0), segment, token_index)
            raw_scores = low_back(jnp.einsum('qhr,kr->hqk', block_queries, keys, precision=HIGHEST))
            scores = jnp.where(allowed[None], raw_scores * score_scale, masked_score)
            softmax_weights = jax.nn.softmax(scores, axis=-1)
            return low(low_back(jnp.einsum('hqk,kr->qhr', low(softmax_weights), latent, precision=HIGHEST)))
        mixed_latent = lax.map(jax.checkpoint(attend), jnp.arange(TREE // block_rows, dtype=jnp.int32)).reshape(TREE, H, R)
        heads_out = low(low_back(jnp.einsum('thr,rhd->thd', mixed_latent, up_heads[:, :, DN:], precision=HIGHEST))).reshape(TREE, H * DV)
        residual = tree_input + low_back(matmul(heads_out, output_weight))
        normed_two = low(rms_norm(residual, second_norm_scale))
        router_probs = jax.nn.softmax(matmul(normed_two, router_weight), axis=-1)
        gates = jnp.take_along_axis(router_probs, tree_routes, axis=1)
        shared_hidden = low(jax.nn.silu(low_back(matmul(normed_two, shared_gate_weight))) * low_back(matmul(normed_two, shared_up_weight)))
        shared_part = matmul(shared_hidden, shared_down_weight)

        def expert_step(routed_total, expert_module):
            chosen = tree_routes == expert_module
            routed = jnp.any(chosen, axis=1)
            weight = lax.optimization_barrier(jnp.sum(jnp.where(chosen, gates, 0.0), axis=1))
            row_order = jnp.argsort(jnp.where(routed, 0, 1).astype(jnp.int32), stable=True)[:most_rows].astype(jnp.int32)
            rows_in = jnp.take(normed_two, row_order, axis=0)
            gate_matrix = jnp.take(expert_gate_weight, expert_module, axis=0)
            upward_matrix = jnp.take(expert_up_weight, expert_module, axis=0)
            down_matrix = jnp.take(expert_down_weight, expert_module, axis=0)
            result = jnp.zeros((most_rows, D), jnp.float32)
            for slice_index in range(N_TENSOR):
                column_start = slice_index * slice_width
                sent = low_back(rows_in)
                gate_pre = low_back(matmul(sent, gate_matrix[:, column_start:column_start + slice_width]))
                up_pre = low_back(matmul(sent, upward_matrix[:, column_start:column_start + slice_width]))
                hidden = low(jax.nn.silu(gate_pre) * up_pre)
                result = result + low(low_back(matmul(hidden, down_matrix[column_start:column_start + slice_width, :])))
            factor = jnp.take(jnp.where(routed, weight, 0.0), row_order, axis=0)
            return (routed_total.at[row_order].add(result * factor[:, None]), None)
        routed_total, unused = lax.scan(jax.checkpoint(expert_step), jnp.zeros((TREE, D), jnp.float32), jnp.arange(EXPERTS, dtype=jnp.int32))
        return residual + shared_part + routed_total
    weight_sequence = tuple((argument.astype(jnp.float32) for argument in (norm_gain, query_proj, latent_proj, latent_gain, latent_up, output_proj, ffn_gain, router, shared_gate, shared_up, shared_down, expert_gate, expert_up, expert_down)))
    route_trees = routes.reshape(tree_count, TREE, TOP)

    def forward(tree_inputs, weights_now):

        def one_tree(pair):
            return jax.checkpoint(tree_forward)(weights_now, pair[0], pair[1])
        return lax.map(one_tree, (tree_inputs, route_trees))
    outputs, pullback = jax.vjp(forward, layer_in.astype(jnp.float32).reshape(tree_count, TREE, D), weight_sequence)
    grad_inputs, grad_weights = pullback(grad_out.astype(jnp.float32).reshape(tree_count, TREE, D))
    return (outputs.reshape(TOKENS, D).astype(jnp.bfloat16), grad_inputs.reshape(TOKENS, D), grad_weights[0], grad_weights[1], grad_weights[2], grad_weights[3], grad_weights[4], grad_weights[5], grad_weights[6], grad_weights[7], grad_weights[8], grad_weights[9], grad_weights[10], grad_weights[11], grad_weights[12], grad_weights[13])
```

```python
import functools

import jax
import jax.numpy as jnp
from jax import lax
from jax.experimental import pallas as pl
from jax.experimental.pallas import tpu as pltpu
from jax.sharding import PartitionSpec as P

D = 2048
DN = 128
DR = 64
DV = 128
R = 512
EXPERTS = 16
NB = 4
NL = 2
LANES = 128

epsilon = 1e-06
masked_score = -1e30
bf16 = jnp.bfloat16
f32 = jnp.float32


def mm(left, right):
    return jnp.dot(left, right, preferred_element_type=f32)


def mm_nt(left, right):
    return lax.dot_general(left, right, (((1,), (1,)), ((), ())), preferred_element_type=f32)


def mm_tn(left, right):
    return lax.dot_general(left, right, (((0,), (0,)), ((), ())), preferred_element_type=f32)


def rms_stats(values):
    return lax.rsqrt(jnp.mean(values * values, axis=-1, keepdims=True) + epsilon)


def rms_back(grad_normed, unit_rows, inverse):
    return inverse * (
        grad_normed - unit_rows * jnp.mean(grad_normed * unit_rows, axis=-1, keepdims=True)
    )


def rotate(values, cosine, sine):
    half_width = values.shape[-1] // 2
    first_half = values[..., :half_width]
    second_half = values[..., half_width:]
    return jnp.concatenate(
        [first_half * cosine - second_half * sine, second_half * cosine + first_half * sine],
        axis=-1,
    )


def rotate_back(grads_in, cosine, sine):
    half_width = grads_in.shape[-1] // 2
    first_half = grads_in[..., :half_width]
    second_half = grads_in[..., half_width:]
    return jnp.concatenate(
        [first_half * cosine + second_half * sine, second_half * cosine - first_half * sine],
        axis=-1,
    )


def tree_layout(leaf_parent, token_index, trunk_len, seg_len):
    beyond = token_index - trunk_len
    in_trunk = token_index < trunk_len
    in_branch = (beyond >= 0) & (beyond < NB * seg_len)
    in_leaf = beyond >= NB * seg_len
    leaf_offset = beyond - NB * seg_len
    leaf_index = jnp.clip(leaf_offset // seg_len, 0, NB * NL - 1)
    position = jnp.where(
        in_trunk,
        token_index,
        jnp.where(
            in_branch, trunk_len + beyond % seg_len, trunk_len + seg_len + leaf_offset % seg_len
        ),
    )
    segment = jnp.where(
        in_trunk, 0, jnp.where(in_branch, 1 + beyond // seg_len, 1 + NB + leaf_index)
    )
    leaf_match = (leaf_index[:, None] == jnp.arange(NB * NL, dtype=jnp.int32)[None, :]).astype(
        jnp.int32
    )
    branch_of_leaf = 1 + jnp.sum(leaf_match * leaf_parent[None, :], axis=1)
    parent = jnp.where(in_trunk, -1, jnp.where(in_branch, 0, branch_of_leaf))
    grand = jnp.where(in_leaf, 0, -1)
    return (position, segment, parent, grand.astype(jnp.int32))


def visible(query_segment, query_parent, query_grand, query_index, key_segment, key_index):
    same_segment = (query_segment[:, None] == key_segment[None, :]) & (
        key_index[None, :] <= query_index[:, None]
    )
    ancestor = (key_segment[None, :] == query_parent[:, None]) | (
        key_segment[None, :] == query_grand[:, None]
    )
    return same_segment | ancestor


def swap(values, axis, step):
    return lax.ppermute(values, axis, [(k, k ^ step) for k in range(lax.axis_size(axis))])


def gather_rel(values, axis):
    size = lax.axis_size(axis)
    if size <= 4:
        return [values] + [swap(values, axis, s) for s in range(1, size)]
    full = lax.all_gather(values, axis)
    me = lax.axis_index(axis)
    return [lax.dynamic_index_in_dim(full, me ^ s, 0, False) for s in range(size)]


def exchange_rel(pieces, axis, stride=1):
    size = lax.axis_size(axis)
    if size <= 4:
        return [pieces[0]] + [swap(p, axis, k * stride) for k, p in enumerate(pieces) if k]
    me = lax.axis_index(axis)
    zero = jnp.zeros_like(pieces[0])
    full = jnp.stack([pieces[s // stride] if s % stride == 0 else zero for s in range(size)])
    order = me ^ jnp.arange(size)
    sent = lax.all_to_all(jnp.take(full, order, axis=0), axis, 0, 0, tiled=True)
    back = jnp.take(sent, order, axis=0)
    return [back[k * stride] for k in range(len(pieces))]


def canonical(pieces, me):
    stacked = jnp.stack(pieces)
    return [lax.dynamic_index_in_dim(stacked, me ^ c, 0, False) for c in range(len(pieces))]


def permute_blocks(values, me, count):
    width = values.shape[-1] // count
    return jnp.concatenate(
        [
            lax.dynamic_slice_in_dim(values, (me ^ s) * width, width, values.ndim - 1)
            for s in range(count)
        ],
        axis=-1,
    )


def total(pieces):
    result = pieces[0].astype(f32)
    for piece in pieces[1:]:
        result = result + piece.astype(f32)
    return result


def halves(own, other, core, dim):
    return jnp.where(
        core == 0,
        jnp.concatenate([own, other], axis=dim),
        jnp.concatenate([other, own], axis=dim),
    )


def pick_half(values, which, dim):
    width = values.shape[dim] // 2
    return lax.dynamic_slice_in_dim(values, which * width, width, dim)


def gather_shared(values, axis, core, dim):
    mine = gather_rel(pick_half(values, core, dim), axis)
    return [values] + [halves(p, swap(p, "tensor", 1), core, dim) for p in mine[1:]]


def after(value, *others):
    return lax.optimization_barrier((value,) + others)[0]


def gather_dp(values):
    if lax.axis_size("dp") != 4:
        return gather_rel(values, "dp")
    cut = values.shape[0] // 2
    first, second = swap(values, "dp", 1), swap(values, "dp", 2)
    last = jnp.concatenate(
        [swap(first[:cut], "dp", 2), swap(second[cut:], "dp", 1)], axis=0
    )
    return [values, first, second, last]


def reduce_dp(pieces):
    if lax.axis_size("dp") != 4:
        return total(exchange_rel(pieces, "dp")).astype(bf16)
    cut = pieces[0].shape[0] // 2
    low, high = [p[:cut] for p in pieces], [p[cut:] for p in pieces]
    low_there, high_there = swap(low[3], "dp", 1), swap(high[3], "dp", 2)
    low_here, high_here = swap(low[1], "dp", 1), swap(high[2], "dp", 2)
    low_next = swap((low[2].astype(f32) + low_there.astype(f32)).astype(bf16), "dp", 2)
    high_next = swap((high[1].astype(f32) + high_there.astype(f32)).astype(bf16), "dp", 1)
    return jnp.concatenate(
        [
            total([low[0], low_here, low_next]).astype(bf16),
            total([high[0], high_here, high_next]).astype(bf16),
        ],
        axis=0,
    )


def gather_z(own_half):
    return jnp.concatenate(gather_rel(own_half, "expert")[1:], axis=0)


def spread_all(own_half, others):
    own_pieces = gather_dp(own_half)
    own_there = swap(jnp.concatenate(own_pieces, axis=0), "tensor", 1)
    other_pieces = gather_dp(others)
    rows, many = own_half.shape[0], others.shape[0]
    near = swap(jnp.concatenate(other_pieces[1:3], axis=0), "tensor", 1)
    other_there = [
        swap(other_pieces[0], "tensor", 1),
        near[:many],
        near[many:],
        swap(other_pieces[3], "tensor", 1),
    ]
    mine, there = [], []
    for s in range(4):
        mine += [other_pieces[s], own_pieces[s]]
        there += [other_there[s], own_there[s * rows : (s + 1) * rows]]
    return jnp.concatenate(mine, axis=0), jnp.concatenate(there, axis=0)


def along_z(others, own):
    tok = own.shape[0]
    count = others.shape[0] // tok
    pieces = [own] + [others[s * tok : (s + 1) * tok] for s in range(count)]
    return total(exchange_rel(pieces, "expert"))


def scatter_all(joined, tok):
    size_dp = lax.axis_size("dp")
    rows = joined.shape[0] // size_dp
    many = rows - tok
    others = reduce_dp([joined[s * rows : s * rows + many] for s in range(size_dp)])
    own = reduce_dp(
        after([joined[s * rows + many : (s + 1) * rows] for s in range(size_dp)], others)
    )
    return along_z(others, own), others


def feed_kernel(sh_width, width, padded, at, n_own, n_oth, g_own, g_oth, wp_own, wp_oth,
                wd_own, wd_oth, hid_out, back_out):
    half = n_own.shape[1]
    rows = n_own.shape[0]
    lane = lax.broadcasted_iota(jnp.int32, (rows, LANES), 1)
    is_router = (lane >= sh_width) & (lane < sh_width + EXPERTS)
    is_own = lane == at[0]

    pre = mm_nt(n_own[...], wp_own[...]) + mm_nt(n_oth[...], wp_oth[...])
    back = mm_nt(g_own[:, :half], wd_own[...]) + mm_nt(g_oth[:, :half], wd_oth[...])
    gate_pre, up_pre = pre[:, :padded], pre[:, padded:]
    logits = jnp.where(is_router, up_pre[:, :LANES], masked_score)
    exps = jnp.exp(logits - jnp.max(logits, axis=1, keepdims=True))
    probs = exps / jnp.sum(exps, axis=1, keepdims=True)
    prob_own = jnp.sum(jnp.where(is_own, probs, 0.0), axis=1, keepdims=True)
    mask = g_own[:, half:].astype(f32)
    routed = jnp.sum(jnp.where(is_own, mask, 0.0), axis=1, keepdims=True)
    gate = routed * prob_own

    def activate(pre, up, back):
        sigmoid = 1.0 / (1.0 + jnp.exp(-pre))
        silu = pre * sigmoid
        slope = sigmoid * (1.0 + pre * (1.0 - sigmoid))
        return silu * up, back * up * slope, back * silu

    hid_s, gg_s, gu_s = activate(gate_pre[:, :LANES], up_pre[:, :LANES], back[:, :LANES])
    hid, gg, gu = activate(gate_pre[:, LANES:], up_pre[:, LANES:], back[:, LANES:])
    prob_grad = routed * jnp.sum(hid * back[:, LANES:], axis=1, keepdims=True)
    logit_grad = probs * (jnp.where(is_own, prob_grad, 0.0) - prob_own * prob_grad)
    hid_out[:, :LANES] = hid_s.astype(bf16)
    hid_out[:, LANES:] = (hid * gate).astype(bf16)
    back_out[:, :LANES] = gg_s.astype(bf16)
    back_out[:, LANES:padded] = (gg * gate).astype(bf16)
    back_out[:, padded : padded + LANES] = jnp.where(is_router, logit_grad, gu_s).astype(bf16)
    back_out[:, padded + LANES :] = (gu * gate).astype(bf16)


def feed_call(at, sh_width, width, padded, rows_own, rows_other, grad_own, grad_other, weights):
    tokens, half = rows_own.shape
    tile = 256
    by_rows = lambda m, at: (m, 0)
    fixed = lambda m, at: (0, 0)
    acts = [rows_own, rows_other, grad_own, grad_other]
    return pl.pallas_call(
        functools.partial(feed_kernel, sh_width, width, padded),
        grid_spec=pltpu.PrefetchScalarGridSpec(
            num_scalar_prefetch=1,
            grid=(tokens // tile,),
            in_specs=[pl.BlockSpec((tile, a.shape[1]), by_rows) for a in acts]
            + [pl.BlockSpec(w.shape, fixed, pipeline_mode=pl.Buffered(1)) for w in weights],
            out_specs=[
                pl.BlockSpec((tile, padded), by_rows),
                pl.BlockSpec((tile, 2 * padded), by_rows),
            ],
        ),
        out_shape=[
            jax.ShapeDtypeStruct((tokens, padded), bf16),
            jax.ShapeDtypeStruct((tokens, 2 * padded), bf16),
        ],
        compiler_params=pltpu.CompilerParams(
            dimension_semantics=("arbitrary",), vmem_limit_bytes=52 * 1024 * 1024
        ),
        cost_estimate=pl.CostEstimate(
            flops=12 * tokens * half * padded,
            bytes_accessed=2 * tokens * (4 * half + 3 * padded) + 12 * half * padded,
            transcendentals=tokens * padded,
        ),
    )(at, *acts, *weights)


def place_kernel(at, *refs):
    pieces, outs = refs[:12], refs[12:]
    step = pl.program_id(0)
    for s in range(4):

        @pl.when(step == s)
        def _():
            for k in range(3):
                outs[k][0] = pieces[3 * s + k][...].astype(f32)


def place_call(i, pieces, width):
    cols = pieces[0].shape[1]
    tile = width // 4
    i = jnp.reshape(i, (1,)).astype(jnp.int32)

    def read(s, k):
        return lambda step, r, at: (4 * k + jnp.where(step == s, r, jnp.where(step < s, 0, 3)), 0)

    return pl.pallas_call(
        place_kernel,
        grid_spec=pltpu.PrefetchScalarGridSpec(
            num_scalar_prefetch=1,
            grid=(4, 4),
            in_specs=[
                pl.BlockSpec((tile, cols), read(s, k)) for s in range(4) for k in range(3)
            ],
            out_specs=[
                pl.BlockSpec((1, tile, cols), lambda step, r, at: (at[0] ^ step, r, 0))
                for k in range(3)
            ],
        ),
        out_shape=[jax.ShapeDtypeStruct((4, width, cols), f32) for k in range(3)],
        compiler_params=pltpu.CompilerParams(
            dimension_semantics=("arbitrary", "arbitrary"), vmem_limit_bytes=32 * 1024 * 1024
        ),
        cost_estimate=pl.CostEstimate(
            flops=0, bytes_accessed=3 * 4 * width * cols * 6, transcendentals=0
        ),
    )(i, *[p for p in pieces for k in range(3)])


def per_device(
    layer_in,
    norm_gain,
    query_proj,
    latent_proj,
    latent_gain,
    latent_up,
    output_proj,
    ffn_gain,
    router,
    shared_gate,
    shared_up,
    shared_down,
    expert_gate,
    expert_up,
    expert_down,
    routes,
    leaf_parent,
    grad_out,
):
    tok = layer_in.shape[0]
    n_dp, n_ex = lax.axis_size("dp"), lax.axis_size("expert")
    i, j, core = lax.axis_index("dp"), lax.axis_index("expert"), lax.axis_index("tensor")
    tree_len = tok * n_ex
    seg_len = tree_len // 16
    trunk_len = 4 * seg_len
    block = D // n_dp
    sub = block // n_ex
    heads_local = output_proj.shape[0] // DV
    groups = min(n_ex, heads_local)
    hp = heads_local // groups
    qg = n_ex // groups
    group = j // qg
    n_q = n_ex // qg
    rows_q = tok * n_q
    qw = DN + DR
    uw = DN + DV
    score_scale = (DN + DR) ** (-0.5)

    x_rel = permute_blocks(layer_in, i, n_dp)
    gain_one = permute_blocks(norm_gain.astype(f32), i, n_dp)
    gain_two = permute_blocks(ffn_gain.astype(f32), i, n_dp)
    gain_latent = latent_gain.astype(f32)
    x_pieces = gather_shared(x_rel, "expert", core, 1)
    wq_pieces = gather_dp(lax.dynamic_slice_in_dim(query_proj, group * hp * qw, hp * qw, 1))
    wl_half = pick_half(latent_proj.T, core, 0)
    wl_got = jnp.concatenate(gather_dp(wl_half), axis=1)
    wl = halves(wl_got, swap(wl_got, "tensor", 1), core, 0)
    wq = jnp.concatenate(wq_pieces, axis=0)
    up_rows = R // n_dp
    up_own = lax.dynamic_slice_in_dim(latent_up, group * hp * uw, hp * uw, 1)
    wo_own = lax.dynamic_slice_in_dim(output_proj, group * hp * DV, hp * DV, 0)
    if up_own.shape[1] == wo_own.shape[1]:
        both = jnp.concatenate([wo_own, up_own], axis=0)
        both_pieces = gather_dp(after(both, wq_pieces[3]))
        wo_pieces = [p[: hp * DV] for p in both_pieces]
        up_pieces = [p[hp * DV :] for p in both_pieces]
    else:
        wo_pieces = gather_rel(wo_own, "dp")
        up_pieces = gather_rel(up_own, "dp")
        both_pieces = wo_pieces
    up = jnp.concatenate(canonical(up_pieces, i), axis=0)
    wo = jnp.concatenate(wo_pieces, axis=1)

    half = D // 2
    local_experts = expert_gate.shape[0]
    parts = n_dp // local_experts
    width = expert_gate.shape[2] // parts
    sh_width = shared_gate.shape[1] // (n_dp * n_ex)
    chosen, part_at = i // parts, (i % parts) * width
    expert_id = j * local_experts + chosen
    sh_pieces = []
    for s in range(n_dp):
        at_unit = (j * n_dp + (i ^ s)) * sh_width
        sh_pieces.append(
            jnp.concatenate(
                [
                    lax.dynamic_slice_in_dim(shared_gate, at_unit, sh_width, 1).T,
                    lax.dynamic_slice_in_dim(shared_up, at_unit, sh_width, 1).T,
                    lax.dynamic_slice_in_dim(shared_down, at_unit, sh_width, 0),
                ],
                axis=0,
            )
        )
    sh_pieces = exchange_rel(after(sh_pieces, both_pieces[3]), "dp")
    sh_rows = jnp.concatenate(canonical(sh_pieces, i), axis=1)
    hidden_width = -(-(LANES + width) // LANES) * LANES

    def routed_rows(weight):
        return lax.dynamic_slice(weight, (chosen, part_at, 0), (1, width, D))[0]

    def hidden_rows(shared, routed, extra):
        room = LANES - sh_width - (0 if extra is None else EXPERTS)
        parts_in = [shared] + ([] if extra is None else [extra])
        return jnp.concatenate(
            parts_in
            + [
                jnp.zeros((room, D), bf16),
                routed,
                jnp.zeros((hidden_width - LANES - width, D), bf16),
            ],
            axis=0,
        )

    gate_w = hidden_rows(
        sh_rows[:sh_width], routed_rows(jnp.swapaxes(expert_gate, 1, 2)), None
    )
    up_w = hidden_rows(
        sh_rows[sh_width : 2 * sh_width], routed_rows(jnp.swapaxes(expert_up, 1, 2)), router.T
    )
    down_w = hidden_rows(sh_rows[2 * sh_width :], routed_rows(expert_down), None)
    pre_w = jnp.concatenate([gate_w, up_w], axis=0)
    pre_own, pre_other = pick_half(pre_w, core, 1), pick_half(pre_w, 1 - core, 1)
    down_own, down_other = pick_half(down_w, core, 1), pick_half(down_w, 1 - core, 1)

    lanes = jnp.arange(LANES, dtype=jnp.int32) - sh_width
    route_lanes = jnp.any(routes[:, :, None] == lanes[None, None, :], axis=1).astype(bf16)
    g_half = jnp.concatenate([pick_half(grad_out, core, 1), route_lanes], axis=1)
    g_others = gather_z(after(g_half, x_pieces[-1]))
    g_rows = jnp.concatenate([after(g_others, sh_pieces[-1]), g_half], axis=0)
    grad_own = jnp.concatenate(gather_dp(g_rows), axis=0)
    grad_other = swap(grad_own, "tensor", 1)

    slots = jnp.arange(tree_len, dtype=jnp.int32)
    token_index = (j ^ (slots // tok)) * tok + slots % tok

    def queries_of(values):
        if qg == 1:
            return values
        split = values.reshape((n_q, qg, tok) + values.shape[1:])[:, 0]
        return split.reshape((rows_q,) + values.shape[1:])

    position, segment, parent, grand = tree_layout(leaf_parent, token_index, trunk_len, seg_len)
    freqs = 10000.0 ** (-2.0 * jnp.arange(DR // 2, dtype=f32) / DR)
    angles = position.astype(f32)[:, None] * freqs[None, :]
    cosine, sine = jnp.cos(angles), jnp.sin(angles)
    q_cos, q_sin = queries_of(cosine), queries_of(sine)
    allowed = visible(
        queries_of(segment),
        queries_of(parent),
        queries_of(grand),
        queries_of(token_index),
        segment,
        token_index,
    )

    own_rows = x_rel.astype(f32)
    inverse_one = rms_stats(own_rows)
    unit_one = own_rows * inverse_one
    tree_rows = jnp.concatenate(x_pieces, axis=0).astype(f32)
    normed = (tree_rows * rms_stats(tree_rows) * gain_one).astype(bf16)
    normed_q = queries_of(normed)
    query_all = mm(normed_q, wq)
    latent_all = mm_nt(normed, wl)
    inverse_latent = rms_stats(latent_all[:, :R])
    unit_latent = latent_all[:, :R] * inverse_latent
    latent = (unit_latent * gain_latent).astype(bf16)
    key_rope = rotate(latent_all[:, R:], cosine, sine).astype(bf16)
    keys = jnp.concatenate([latent, key_rope], axis=1)
    up_key = [up[:, h * uw : h * uw + DN] for h in range(hp)]
    up_value = [up[:, h * uw + DN : (h + 1) * uw] for h in range(hp)]
    query_nope = [query_all[:, h * qw : h * qw + DN].astype(bf16) for h in range(hp)]
    queries = jnp.concatenate(
        [
            jnp.concatenate(
                [
                    mm_nt(query_nope[h], up_key[h]).astype(bf16),
                    rotate(query_all[:, h * qw + DN : (h + 1) * qw], q_cos, q_sin).astype(bf16),
                ],
                axis=1,
            )
            for h in range(hp)
        ],
        axis=0,
    )
    raw_scores = mm_nt(queries, keys).reshape(hp, rows_q, tree_len)
    scores = jnp.where(allowed[None], raw_scores * score_scale, masked_score)
    exp_scores = jnp.exp(scores - jnp.max(scores, axis=-1, keepdims=True))
    probs = exp_scores / jnp.sum(exp_scores, axis=-1, keepdims=True)
    probs = probs.reshape(hp * rows_q, tree_len)
    probs_low = probs.astype(bf16)
    mixed = mm(probs_low, latent).astype(bf16)
    mixed_head = [mixed[h * rows_q : (h + 1) * rows_q] for h in range(hp)]
    heads_out = jnp.concatenate(
        [mm(mixed_head[h], up_value[h]).astype(bf16) for h in range(hp)], axis=1
    )
    wo_mine, wo_other = pick_half(wo, core, 1), pick_half(wo, 1 - core, 1)

    def tree_scatter(partial_own, partial_other, count, stride):
        joined = partial_own + swap(partial_other.astype(bf16), "tensor", 1).astype(f32)
        joined = joined.astype(bf16)
        own = total(
            exchange_rel(
                [joined[s * tok : (s + 1) * tok] for s in range(count)], "expert", stride
            )
        )
        return halves(own, swap(own, "tensor", 1), core, 1)

    attention = tree_scatter(mm(heads_out, wo_mine), mm(heads_out, wo_other), n_q, qg)
    residual = own_rows + attention
    inverse_two = rms_stats(residual)
    unit_two = residual * inverse_two
    normed_two = permute_blocks((unit_two * gain_two).astype(bf16), i, n_dp)

    n_half = pick_half(normed_two, core, 1)
    rows_own, rows_other = spread_all(n_half, gather_z(n_half))
    at = jnp.reshape(sh_width + expert_id, (1,)).astype(jnp.int32)
    hidden_scaled, back_pre = feed_call(
        at, sh_width, width, hidden_width, rows_own, rows_other, grad_own, grad_other,
        [pre_own, pre_other, down_own, down_other],
    )

    def join(mine, theirs):
        return (mine.astype(f32) + swap(theirs, "tensor", 1).astype(f32)).astype(bf16)

    rows_theirs = mm(back_pre, pre_other).astype(bf16)
    back_later = after(back_pre, rows_theirs)
    grad_rows = join(mm(back_later, pre_own).astype(bf16), rows_theirs)
    gn2_half, gn2_sent = scatter_all(grad_rows, tok)
    gn2 = permute_blocks(halves(gn2_half, swap(gn2_half, "tensor", 1), core, 1), i, n_dp)

    grad_ffn_gain = jnp.sum(gn2 * unit_two, axis=0, keepdims=True)
    grad_residual = permute_blocks(grad_out, i, n_dp).astype(f32) + rms_back(
        gn2 * gain_two, unit_two, inverse_two
    )

    hidden_late, back_late, _ = lax.optimization_barrier((hidden_scaled, back_pre, grad_rows))
    out_joined = join(
        mm(hidden_late, down_own).astype(bf16), mm(hidden_late, down_other).astype(bf16)
    )
    out_joined = after(out_joined, gn2_sent)
    rows_dp = tokens_dp = out_joined.shape[0] // n_dp
    out_mine = reduce_dp([out_joined[s * rows_dp : (s + 1) * rows_dp] for s in range(n_dp)])
    ffn_half = along_z(out_mine[: rows_dp - tok], out_mine[rows_dp - tok :])
    out_half = (pick_half(permute_blocks(residual, i, n_dp), core, 1) + ffn_half).astype(bf16)
    layer_out = halves(out_half, swap(out_half, "tensor", 1), core, 1)

    def block_offset(c):
        per_half = n_dp // 2
        return ((c // per_half) ^ core) * half + (c % per_half) * block

    def both_halves(left, own, other):
        return jnp.concatenate(
            [mm_tn(left, own).astype(bf16), mm_tn(left, other).astype(bf16)], axis=1
        )

    pre_grads = both_halves(back_late, rows_own, rows_other)
    down_grads = both_halves(hidden_late, grad_own[:, :half], grad_other[:, :half])
    routed_at = slice(LANES, LANES + width)
    up_at = slice(hidden_width + LANES, hidden_width + LANES + width)
    sent_width = -(-sh_width // 16) * 16
    feed_pieces = []
    for s in range(n_dp):
        start = block_offset(i ^ s)
        pre_cut = lax.dynamic_slice_in_dim(pre_grads, start, block, 1)
        down_cut = lax.dynamic_slice_in_dim(down_grads, start, block, 1)
        feed_pieces.append(
            jnp.concatenate(
                [
                    pre_cut[routed_at],
                    pre_cut[up_at],
                    down_cut[routed_at],
                    pre_cut[:sent_width],
                    pre_cut[hidden_width : hidden_width + sent_width],
                    down_cut[:sent_width],
                ],
                axis=0,
            )
        )
    feed_pieces = exchange_rel(after(feed_pieces, out_mine), "dp")
    if parts == 1:
        placed = place_call(i, feed_pieces, width)
    else:
        stacked = jnp.stack(canonical(feed_pieces, i)).astype(f32)
        placed = [
            stacked[:, k * width : (k + 1) * width].reshape(local_experts, parts * width, block)
            for k in range(3)
        ]
    grad_expert_gate = jnp.swapaxes(placed[0], 1, 2)
    grad_expert_up = jnp.swapaxes(placed[1], 1, 2)
    grad_expert_down = placed[2]
    shared_all = jnp.stack(canonical([p[3 * width :] for p in feed_pieces], i))
    shared_all = jnp.stack(
        canonical(
            exchange_rel(
                [lax.dynamic_slice_in_dim(shared_all, (j ^ s) * sub, sub, 2) for s in range(n_ex)],
                "expert",
            ),
            j,
        )
    )

    def shared_part(k):
        rows = shared_all[:, :, k * sent_width : k * sent_width + sh_width]
        return rows.reshape(-1, sub).astype(f32)

    grad_shared_gate, grad_shared_up = shared_part(0).T, shared_part(1).T
    grad_shared_down = shared_part(2)
    router_block = pre_grads[hidden_width + sh_width : hidden_width + sh_width + EXPERTS]
    grad_router_rows = permute_blocks(
        halves(router_block[:, :half], router_block[:, half:], core, 1), i, n_dp
    )

    res_pieces = gather_shared(grad_residual.astype(bf16), "expert", core, 1)
    res_q = jnp.concatenate(res_pieces[::qg], axis=0)
    grad_heads = mm_nt(res_q, wo).astype(bf16)
    grad_head = [grad_heads[:, h * DV : (h + 1) * DV] for h in range(hp)]

    grad_wo = mm_tn(heads_out, res_q)

    grad_mixed = jnp.concatenate(
        [mm_nt(grad_head[h], up_value[h]).astype(bf16) for h in range(hp)], axis=0
    )
    grad_att = mm_nt(grad_mixed, latent)
    delta = jnp.sum(probs * grad_att, axis=-1, keepdims=True)
    score_grad = (probs * (grad_att - delta) * score_scale).astype(bf16)
    grad_queries = mm(score_grad, keys)
    grad_keys = mm_tn(score_grad, queries)
    grad_latent_keys = grad_keys[:, :R] + mm_tn(probs_low, grad_mixed)
    grad_query_latent = grad_queries[:, :R].astype(bf16)
    grad_query_parts, grad_up_parts = [], []
    for h in range(hp):
        rows = slice(h * rows_q, (h + 1) * rows_q)
        grad_query_parts.append(mm(grad_query_latent[rows], up_key[h]))
        grad_query_parts.append(rotate_back(grad_queries[rows, R:], q_cos, q_sin))
        grad_up_parts.append(mm_tn(query_nope[h], grad_query_latent[rows]))
        grad_up_parts.append(mm_tn(grad_head[h], mixed_head[h]))
    grad_query_all = jnp.concatenate(grad_query_parts, axis=1).astype(bf16)
    grad_latent_gain = jnp.sum(grad_latent_keys * unit_latent, axis=0, keepdims=True)
    grad_latent_all = jnp.concatenate(
        [
            rms_back(grad_latent_keys * gain_latent, unit_latent, inverse_latent),
            rotate_back(grad_keys[:, R:], cosine, sine),
        ],
        axis=1,
    ).astype(bf16)

    grad_query_rows = grad_query_all
    if qg > 1:
        grad_query_rows = jnp.pad(
            grad_query_all.reshape(n_q, 1, tok, -1), ((0, 0), (0, qg - 1), (0, 0), (0, 0))
        ).reshape(tree_len, -1)
    back_mine = mm_nt(grad_query_rows, pick_half(wq, core, 0)) + mm(
        grad_latent_all, pick_half(wl, core, 1)
    )
    back_other = mm_nt(grad_query_rows, pick_half(wq, 1 - core, 0)) + mm(
        grad_latent_all, pick_half(wl, 1 - core, 1)
    )
    grad_normed = tree_scatter(back_mine, back_other, n_ex, 1)
    grad_norm_gain = jnp.sum(grad_normed * unit_one, axis=0, keepdims=True)
    grad_in = permute_blocks(
        grad_residual + rms_back(grad_normed * gain_one, unit_one, inverse_one), i, n_dp
    )

    by_d = jnp.concatenate(
        [grad_wo, mm_tn(grad_query_all, normed_q), mm_tn(grad_latent_all, normed)], axis=0
    ).astype(bf16)
    by_r = jnp.concatenate(grad_up_parts, axis=0).astype(bf16)
    d_rows, r_rows = by_d.shape[0], by_r.shape[0]
    by_r = [lax.dynamic_slice_in_dim(by_r, (i ^ s) * up_rows, up_rows, 1) for s in range(n_dp)]
    split_r = block // up_rows
    cut_r = r_rows // split_r
    pieces = [
        jnp.concatenate(
            [by_d[:, s * block : (s + 1) * block]]
            + [jnp.concatenate([by_r[s][c * cut_r : (c + 1) * cut_r] for c in range(split_r)], 1)],
            axis=0,
        )
        for s in range(n_dp)
    ]
    mine = reduce_dp(pieces)
    mine_d = mine[:d_rows]
    mine_r = jnp.concatenate(
        [mine[d_rows:, c * up_rows : (c + 1) * up_rows] for c in range(split_r)], axis=0
    )
    up_sub = up_rows // n_ex
    got_d = exchange_rel(
        [lax.dynamic_slice_in_dim(mine_d, (j ^ s) * sub, sub, 1) for s in range(n_ex)], "expert"
    )
    got_r = exchange_rel(
        [lax.dynamic_slice_in_dim(mine_r, (j ^ s) * up_sub, up_sub, 1) for s in range(n_ex)],
        "expert",
    )

    def over_groups(pieces):
        ordered = canonical(pieces, j)
        return jnp.concatenate(
            [total(ordered[g * qg : (g + 1) * qg]) for g in range(groups)], axis=0
        )

    wo_rows, wq_rows = hp * DV, hp * qw
    grad_output_proj = over_groups([p[:wo_rows] for p in got_d])
    grad_query_proj = over_groups([p[wo_rows : wo_rows + wq_rows] for p in got_d]).T
    grad_latent_up = over_groups(got_r).T
    grad_wl = total([p[wo_rows + wq_rows :] for p in got_d])
    grad_latent_proj = (grad_wl + swap(grad_wl, "tensor", 1)).T

    small_d = jnp.concatenate(
        [0.5 * grad_norm_gain, 0.5 * grad_ffn_gain, grad_router_rows.astype(f32)], axis=0
    )
    small = [
        jnp.concatenate(
            [
                small_d[:, s * block : (s + 1) * block].reshape(-1, n_ex, sub),
                jnp.pad(
                    lax.dynamic_slice_in_dim(
                        grad_latent_gain, (i ^ s) * up_rows, up_rows, 1
                    ).reshape(1, n_ex, up_sub),
                    ((0, 0), (0, 0), (0, sub - up_sub)),
                ),
            ],
            axis=0,
        )
        for s in range(n_dp)
    ]
    small = total(exchange_rel(small, "dp"))
    small = total(
        exchange_rel(
            [lax.dynamic_index_in_dim(small, j ^ s, 1, False) for s in range(n_ex)], "expert"
        )
    )
    small = small + swap(small, "tensor", 1)

    return (
        layer_out,
        grad_in,
        small[0],
        grad_query_proj,
        grad_latent_proj,
        small[2 + EXPERTS, :up_sub],
        grad_latent_up,
        grad_output_proj,
        small[1],
        small[2 : 2 + EXPERTS].T,
        grad_shared_gate,
        grad_shared_up,
        grad_shared_down,
        grad_expert_gate,
        grad_expert_up,
        grad_expert_down,
    )


def solution(mesh):
    placed = (
        P(("dp", "expert"), None),
        P(),
        P("dp", "tensor"),
        P("dp", None),
        P(),
        P("dp", "tensor"),
        P("tensor", "dp"),
        P(),
        P(),
        P("dp", "tensor"),
        P("dp", "tensor"),
        P("tensor", "dp"),
        P("expert", None, "tensor"),
        P("expert", None, "tensor"),
        P("expert", "tensor", None),
        P(("dp", "expert"), None),
        P(),
        P(("dp", "expert"), None),
    )
    return jax.shard_map(
        per_device,
        mesh=mesh,
        in_specs=placed,
        out_specs=(
            P(("dp", "expert"), None),
            P(("dp", "expert"), None),
            P(("dp", "expert")),
            P(("dp", "expert"), "tensor"),
            P(("dp", "expert"), None),
            P(("dp", "expert")),
            P(("dp", "expert"), "tensor"),
            P("tensor", ("dp", "expert")),
            P(("dp", "expert")),
            P(("dp", "expert"), None),
            P(("dp", "expert"), "tensor"),
            P(("dp", "expert"), "tensor"),
            P("tensor", ("dp", "expert")),
            P("expert", "dp", "tensor"),
            P("expert", "dp", "tensor"),
            P("expert", "tensor", "dp"),
        ),
        check_vma=False,
    )
```

```python
import functools

import jax
import jax.numpy as jnp
from jax import lax
from jax.experimental import pallas as pl
from jax.experimental.pallas import tpu as pltpu
from jax.sharding import PartitionSpec as P

D = 2048
DN = 128
DR = 64
DV = 128
R = 512
EXPERTS = 16
NB = 4
NL = 2
LANES = 128

epsilon = 1e-06
masked_score = -1e30
bf16 = jnp.bfloat16
f32 = jnp.float32


def mm(left, right):
    return jnp.dot(left, right, preferred_element_type=f32)


def mm_nt(left, right):
    return lax.dot_general(left, right, (((1,), (1,)), ((), ())), preferred_element_type=f32)


def mm_tn(left, right):
    return lax.dot_general(left, right, (((0,), (0,)), ((), ())), preferred_element_type=f32)


def rms_stats(values):
    return lax.rsqrt(jnp.mean(values * values, axis=-1, keepdims=True) + epsilon)


def rms_back(grad_normed, unit_rows, inverse):
    return inverse * (
        grad_normed - unit_rows * jnp.mean(grad_normed * unit_rows, axis=-1, keepdims=True)
    )


def rotate(values, cosine, sine):
    half_width = values.shape[-1] // 2
    first_half = values[..., :half_width]
    second_half = values[..., half_width:]
    return jnp.concatenate(
        [first_half * cosine - second_half * sine, second_half * cosine + first_half * sine],
        axis=-1,
    )


def rotate_back(grads_in, cosine, sine):
    half_width = grads_in.shape[-1] // 2
    first_half = grads_in[..., :half_width]
    second_half = grads_in[..., half_width:]
    return jnp.concatenate(
        [first_half * cosine + second_half * sine, second_half * cosine - first_half * sine],
        axis=-1,
    )


def tree_layout(leaf_parent, token_index, trunk_len, seg_len):
    beyond = token_index - trunk_len
    in_trunk = token_index < trunk_len
    in_branch = (beyond >= 0) & (beyond < NB * seg_len)
    in_leaf = beyond >= NB * seg_len
    leaf_offset = beyond - NB * seg_len
    leaf_index = jnp.clip(leaf_offset // seg_len, 0, NB * NL - 1)
    position = jnp.where(
        in_trunk,
        token_index,
        jnp.where(
            in_branch, trunk_len + beyond % seg_len, trunk_len + seg_len + leaf_offset % seg_len
        ),
    )
    segment = jnp.where(
        in_trunk, 0, jnp.where(in_branch, 1 + beyond // seg_len, 1 + NB + leaf_index)
    )
    leaf_match = (leaf_index[:, None] == jnp.arange(NB * NL, dtype=jnp.int32)[None, :]).astype(
        jnp.int32
    )
    branch_of_leaf = 1 + jnp.sum(leaf_match * leaf_parent[None, :], axis=1)
    parent = jnp.where(in_trunk, -1, jnp.where(in_branch, 0, branch_of_leaf))
    grand = jnp.where(in_leaf, 0, -1)
    return (position, segment, parent, grand.astype(jnp.int32))


def visible(query_segment, query_parent, query_grand, query_index, key_segment, key_index):
    same_segment = (query_segment[:, None] == key_segment[None, :]) & (
        key_index[None, :] <= query_index[:, None]
    )
    ancestor = (key_segment[None, :] == query_parent[:, None]) | (
        key_segment[None, :] == query_grand[:, None]
    )
    return same_segment | ancestor


def swap(values, axis, step):
    return lax.ppermute(values, axis, [(k, k ^ step) for k in range(lax.axis_size(axis))])


def gather_rel(values, axis):
    size = lax.axis_size(axis)
    if size <= 4:
        return [values] + [swap(values, axis, s) for s in range(1, size)]
    full = lax.all_gather(values, axis)
    me = lax.axis_index(axis)
    return [lax.dynamic_index_in_dim(full, me ^ s, 0, False) for s in range(size)]


def exchange_rel(pieces, axis, stride=1):
    size = lax.axis_size(axis)
    if size <= 4:
        return [pieces[0]] + [swap(p, axis, k * stride) for k, p in enumerate(pieces) if k]
    me = lax.axis_index(axis)
    zero = jnp.zeros_like(pieces[0])
    full = jnp.stack([pieces[s // stride] if s % stride == 0 else zero for s in range(size)])
    order = me ^ jnp.arange(size)
    sent = lax.all_to_all(jnp.take(full, order, axis=0), axis, 0, 0, tiled=True)
    back = jnp.take(sent, order, axis=0)
    return [back[k * stride] for k in range(len(pieces))]


def canonical(pieces, me):
    stacked = jnp.stack(pieces)
    return [lax.dynamic_index_in_dim(stacked, me ^ c, 0, False) for c in range(len(pieces))]


def permute_blocks(values, me, count):
    width = values.shape[-1] // count
    return jnp.concatenate(
        [
            lax.dynamic_slice_in_dim(values, (me ^ s) * width, width, values.ndim - 1)
            for s in range(count)
        ],
        axis=-1,
    )


def total(pieces):
    result = pieces[0].astype(f32)
    for piece in pieces[1:]:
        result = result + piece.astype(f32)
    return result


def halves(own, other, core, dim):
    return jnp.where(
        core == 0,
        jnp.concatenate([own, other], axis=dim),
        jnp.concatenate([other, own], axis=dim),
    )


def pick_half(values, which, dim):
    width = values.shape[dim] // 2
    return lax.dynamic_slice_in_dim(values, which * width, width, dim)


def gather_shared(values, axis, core, dim):
    mine = gather_rel(pick_half(values, core, dim), axis)
    return [values] + [halves(p, swap(p, "tensor", 1), core, dim) for p in mine[1:]]


def keep_kernel(*refs):
    pass


def order(values, others):
    count, total_count = len(values), len(values) + len(others)
    anywhere = pl.BlockSpec(memory_space=pl.ANY)
    return pl.pallas_call(
        keep_kernel,
        in_specs=[anywhere] * total_count,
        out_specs=[anywhere] * count,
        out_shape=[jax.ShapeDtypeStruct(v.shape, v.dtype) for v in values],
        input_output_aliases={k: k for k in range(count)},
        cost_estimate=pl.CostEstimate(flops=0, bytes_accessed=0, transcendentals=0),
    )(*values, *others)


def place_rows(parts, rows, others=()):
    spans = [p[5] if len(p) > 5 else (0, p[0].shape[1]) for p in parts]
    columns = max(part[4] + span[1] for part, span in zip(parts, spans))

    def body(*refs):
        out, sems = refs[-2], refs[-1]
        copies = []
        for k, part in enumerate(parts):
            source = refs[k].at[pl.ds(part[1], part[2]), pl.ds(*spans[k])]
            target = out.at[pl.ds(part[3], part[2]), pl.ds(part[4], spans[k][1])]
            copies.append(pltpu.make_async_copy(source, target, sems.at[k]))
        for copy in copies:
            copy.start()
        for copy in copies:
            copy.wait()

    anywhere = pl.BlockSpec(memory_space=pl.ANY)
    return pl.pallas_call(
        body,
        in_specs=[anywhere] * (len(parts) + len(others)),
        out_specs=pl.BlockSpec(memory_space=pltpu.VMEM),
        out_shape=jax.ShapeDtypeStruct((rows, columns), parts[0][0].dtype),
        scratch_shapes=[pltpu.SemaphoreType.DMA((len(parts),))],
        compiler_params=pltpu.CompilerParams(vmem_limit_bytes=48 * 1024 * 1024),
        cost_estimate=pl.CostEstimate(flops=0, bytes_accessed=0, transcendentals=0),
    )(*[part[0] for part in parts], *others)


def pack_kernel(at, query, latent, up, out_w, packed):
    turned = query[...].T
    rows = DN + DR
    packed[0:DN] = turned[:DN]
    packed[DN : 2 * DN] = turned[rows : rows + DN]
    packed[2 * DN : 2 * DN + DR] = turned[DN:rows]
    packed[2 * DN + DR : 2 * rows] = turned[rows + DN :]
    first = 2 * rows
    for ref in (latent, up, out_w):
        packed[first : first + ref.shape[0]] = ref[...]
        first += ref.shape[0]


def pack_call(at, query_proj, latent_t, latent_up, output_proj, wide):
    block = query_proj.shape[0]
    qw, uw = 2 * (DN + DR), 2 * (DN + DV)
    sizes = [qw, latent_t.shape[0] // 2, latent_up.shape[0], 2 * DV]
    return pl.pallas_call(
        pack_kernel,
        grid_spec=pltpu.PrefetchScalarGridSpec(
            num_scalar_prefetch=1,
            grid=(1,),
            in_specs=[
                pl.BlockSpec((block, qw), lambda m, at: (0, at[0])),
                pl.BlockSpec((sizes[1], block), lambda m, at: (at[1], 0)),
                pl.BlockSpec((sizes[2], uw), lambda m, at: (0, at[0])),
                pl.BlockSpec((sizes[3], block), lambda m, at: (at[0], 0)),
            ],
            out_specs=pl.BlockSpec((sum(sizes), block), lambda m, at: (0, 0)),
        ),
        out_shape=jax.ShapeDtypeStruct((sum(sizes), block), bf16),
        compiler_params=pltpu.CompilerParams(vmem_limit_bytes=24 * 1024 * 1024),
        cost_estimate=pl.CostEstimate(flops=0, bytes_accessed=0, transcendentals=0),
    )(at, query_proj, latent_t, latent_up, output_proj)


def join_rows(arrays, others=()):
    parts, at = [], 0
    for array in arrays:
        parts.append((array, 0, array.shape[0], at, 0))
        at += array.shape[0]
    return place_rows(parts, at, others)


def gather_parts(values, between=None):
    if lax.axis_size("dp") != 4:
        return [[p] for p in gather_rel(values, "dp")]
    cut = values.shape[0] // 2
    first, second = swap(values, "dp", 1), swap(values, "dp", 2)
    low, high = first[:cut], second[cut:]
    if between is not None:
        low, high = order([low, high], between)
    return [[values], [first], [second], [swap(low, "dp", 2), swap(high, "dp", 1)]]


def gather_dp(values, between=None):
    return [p[0] if len(p) == 1 else join_rows(p) for p in gather_parts(values, between)]


def stack_kernel(*refs):
    at = 0
    for ref in refs[:-1]:
        refs[-1][at : at + ref.shape[0]] = ref[...].astype(bf16)
        at += ref.shape[0]


def stack_rows(parts, block):
    rows, columns = sum(p.shape[0] for p in parts), parts[0].shape[1]
    made = pl.pallas_call(
        stack_kernel,
        grid=(columns // block,),
        in_specs=[pl.BlockSpec((p.shape[0], block), lambda c: (0, c)) for p in parts],
        out_specs=pl.BlockSpec((rows, block), lambda c: (c, 0)),
        out_shape=jax.ShapeDtypeStruct((rows * (columns // block), block), bf16),
        compiler_params=pltpu.CompilerParams(vmem_limit_bytes=32 * 1024 * 1024),
        cost_estimate=pl.CostEstimate(flops=0, bytes_accessed=8 * rows * columns, transcendentals=0),
    )(*parts)
    return [made[c * rows : (c + 1) * rows] for c in range(columns // block)]


def reduce_first(pieces):
    cut = pieces[0].shape[0] // 2
    low, high = [p[:cut] for p in pieces], [p[cut:] for p in pieces]
    low_got = swap(jnp.concatenate([low[1], low[3]], axis=0), "dp", 1)
    high_got = swap(jnp.concatenate([high[2], high[3]], axis=0), "dp", 2)
    return low, high, low_got, high_got


def reduce_second(state, between=None):
    low, high, low_got, high_got = state
    cut = low[0].shape[0]
    low_sum = (low[2].astype(f32) + low_got[cut:].astype(f32)).astype(bf16)
    high_sum = (high[1].astype(f32) + high_got[cut:].astype(f32)).astype(bf16)
    if between is not None:
        low_sum, high_sum = order([low_sum, high_sum], between)
    low_next, high_next = swap(low_sum, "dp", 2), swap(high_sum, "dp", 1)
    return jnp.concatenate(
        [
            total([low[0], low_got[:cut], low_next]).astype(bf16),
            total([high[0], high_got[:cut], high_next]).astype(bf16),
        ],
        axis=0,
    )


def gather_z(own_half):
    return jnp.concatenate(gather_rel(own_half, "expert")[1:], axis=0)


def along_z(others, own):
    tok = own.shape[0]
    count = others.shape[0] // tok
    pieces = [own] + [others[s * tok : (s + 1) * tok] for s in range(count)]
    return total(exchange_rel(pieces, "expert"))


def rows_join(own, other, core):
    rows = own.shape[0]
    result = jnp.zeros((2 * rows,) + own.shape[1:], own.dtype)
    result = lax.dynamic_update_slice_in_dim(result, own, core * rows, 0)
    return lax.dynamic_update_slice_in_dim(result, other, (1 - core) * rows, 0)


def feed_kernel(sh_width, width, padded, sub, at, n_own, n_oth, g_own, g_oth, gate_hbm, up_hbm, down_hbm,
                shared_hbm, *refs):
    hid_out, back_out, rows_own, rows_oth, out_own, out_oth, pre_w, down_w, sems = refs[-9:]
    half = n_own.shape[1]

    @pl.when(pl.program_id(0) == 0)
    def _():
        pick, core = at[0], at[1]
        copies = []
        for k in range(2):
            here = pl.multiple_of((core if k == 0 else 1 - core) * half, LANES)
            cols, to = pl.ds(here, half), pl.ds(k * half, half)
            moves = [
                (gate_hbm.at[pick, :, cols], pre_w.at[pl.ds(LANES, width), to]),
                (up_hbm.at[pick, :, cols], pre_w.at[pl.ds(padded + LANES, width), to]),
                (down_hbm.at[pick, :, cols], down_w.at[pl.ds(LANES, width), to]),
                (shared_hbm.at[pl.ds(0, LANES), cols], pre_w.at[pl.ds(0, LANES), to]),
                (shared_hbm.at[pl.ds(LANES, LANES), cols], pre_w.at[pl.ds(padded, LANES), to]),
                (shared_hbm.at[pl.ds(2 * LANES, LANES), cols], down_w.at[pl.ds(0, LANES), to]),
            ]
            for m, (source, target) in enumerate(moves):
                copies.append(pltpu.make_async_copy(source, target, sems.at[6 * k + m]))
        for copy in copies:
            copy.start()
        room = padded - LANES - width
        if room:
            zeros = jnp.zeros((room, 2 * half), bf16)
            pre_w[pl.ds(LANES + width, room), :] = zeros
            pre_w[pl.ds(padded + LANES + width, room), :] = zeros
            down_w[pl.ds(LANES + width, room), :] = zeros
        for copy in copies:
            copy.wait()

    lane = lax.broadcasted_iota(jnp.int32, (sub, LANES), 1)
    is_router = (lane >= sh_width) & (lane < sh_width + EXPERTS)
    is_own = lane == at[2]

    def activate(pre, up, back):
        sigmoid = 1.0 / (1.0 + jnp.exp(-pre))
        silu = pre * sigmoid
        slope = sigmoid + silu * (1.0 - sigmoid)
        return silu * up, back * up * slope, back * silu

    for start in range(0, n_own.shape[0], sub):
        rows = slice(start, start + sub)
        pre = mm_nt(n_own[rows], pre_w[:, :half]) + mm_nt(n_oth[rows], pre_w[:, half:])
        back = mm_nt(g_own[rows, :half], down_w[:, :half])
        back = back + mm_nt(g_oth[rows, :half], down_w[:, half:])
        gate_pre, up_pre = pre[:, :padded], pre[:, padded:]
        logits = jnp.where(is_router, up_pre[:, :LANES], masked_score)
        exps = jnp.exp(logits - jnp.max(logits, axis=1, keepdims=True))
        probs = exps / jnp.sum(exps, axis=1, keepdims=True)
        prob_own = jnp.sum(jnp.where(is_own, probs, 0.0), axis=1, keepdims=True)
        mask = g_own[rows, half:].astype(f32)
        routed = jnp.sum(jnp.where(is_own, mask, 0.0), axis=1, keepdims=True)
        gate = routed * prob_own
        hid_s, gg_s, gu_s = activate(gate_pre[:, :LANES], up_pre[:, :LANES], back[:, :LANES])
        hid, gg, gu = activate(gate_pre[:, LANES:], up_pre[:, LANES:], back[:, LANES:])
        prob_grad = routed * jnp.sum(hid * back[:, LANES:], axis=1, keepdims=True)
        logit_grad = probs * (jnp.where(is_own, prob_grad, 0.0) - prob_own * prob_grad)
        hid_out[rows, :LANES] = hid_s.astype(bf16)
        hid_out[rows, LANES:] = (hid * gate).astype(bf16)
        back_out[rows, :LANES] = gg_s.astype(bf16)
        back_out[rows, LANES:padded] = (gg * gate).astype(bf16)
        back_out[rows, padded : padded + LANES] = jnp.where(is_router, logit_grad, gu_s).astype(bf16)
        back_out[rows, padded + LANES :] = (gu * gate).astype(bf16)
        rows_oth[rows] = mm(back_out[rows], pre_w[:, half:]).astype(bf16)
        rows_own[rows] = mm(back_out[rows], pre_w[:, :half]).astype(bf16)
        out_oth[rows] = mm(hid_out[rows], down_w[:, half:]).astype(bf16)
        out_own[rows] = mm(hid_out[rows], down_w[:, :half]).astype(bf16)


def feed_call(at, sh_width, width, padded, rows_own, rows_other, grad_own, grad_other, weights, place, kept, others):
    tokens, half = rows_own.shape
    tile, sub = 256, 256
    by_rows = lambda m, at: (m, 0)
    first, every = place[0] // tile, place[1]
    placed_rows = lambda m, at: (m + first, 0)
    acts = [rows_own, rows_other, grad_own, grad_other]
    widths = [padded, 2 * padded, half, half, half, half]
    return pl.pallas_call(
        functools.partial(feed_kernel, sh_width, width, padded, sub),
        grid_spec=pltpu.PrefetchScalarGridSpec(
            num_scalar_prefetch=1,
            grid=(tokens // tile,),
            in_specs=[pl.BlockSpec((tile, a.shape[1]), by_rows) for a in acts]
            + [pl.BlockSpec(memory_space=pl.ANY) for w in weights + kept + others],
            out_specs=[
                pl.BlockSpec((tile, w), placed_rows if k < 2 else by_rows)
                for k, w in enumerate(widths)
            ],
            scratch_shapes=[
                pltpu.VMEM((2 * padded, 2 * half), bf16),
                pltpu.VMEM((padded, 2 * half), bf16),
                pltpu.SemaphoreType.DMA((12,)),
            ],
        ),
        out_shape=[
            jax.ShapeDtypeStruct((every if k < 2 else tokens, w), bf16)
            for k, w in enumerate(widths)
        ],
        input_output_aliases={9 + k: k for k in range(len(kept))},
        compiler_params=pltpu.CompilerParams(
            dimension_semantics=("arbitrary",), vmem_limit_bytes=58 * 1024 * 1024
        ),
        cost_estimate=pl.CostEstimate(
            flops=24 * tokens * half * padded,
            bytes_accessed=2 * tokens * (8 * half + 3 * padded) + 12 * half * padded,
            transcendentals=tokens * padded,
        ),
    )(at, *acts, *weights, *kept, *others)


def swap_quarters(values):
    lane = lax.broadcasted_iota(jnp.int32, values.shape, 1)
    return jnp.where(lane % 64 < 32, pltpu.roll(values, 96, 1), pltpu.roll(values, 32, 1))


def assemble(at, sources, x, wq, wl, up, wo, sems):
    x_rel, x_got, x_there, wl_there = sources[0], sources[1:4], sources[4:7], sources[7]
    pieces = [[sources[8]], [sources[9]], [sources[10]], list(sources[11:])]
    core, index = at[0], at[1]
    block = sources[8].shape[1]
    half, own, wl_rows = D // 2, x_rel.shape[0], wl_there.shape[0]
    up_rows = R // 4
    copies = []

    def copy(source, target):
        copies.append(pltpu.make_async_copy(source, target, sems.at[len(copies)]))

    def columns(which):
        return pl.ds(pl.multiple_of(which * half, LANES), half)

    def rows(first, unit, count):
        return pl.ds(pl.multiple_of(first * unit, 16), count)

    copy(x_rel, x.at[pl.ds(0, own)])
    for k in range(3):
        to = pl.ds((k + 1) * own, own)
        copy(x_got[k].at[:, pl.ds(0, half)], x.at[to, columns(core)])
        copy(x_there[k].at[:, pl.ds(0, half)], x.at[to, columns(1 - core)])
    copy(wl_there, wl.at[rows(1 - core, wl_rows, wl_rows)])
    fields = [wq.shape[0], wl_rows, up_rows, 0 if wo is None else wo.shape[0]]
    for s, parts in enumerate(pieces):
        base = 0
        for part in parts:
            start = 0
            for f, size in enumerate(fields):
                first, last = max(start, base), min(start + size, base + part.shape[0])
                if first < last:
                    source = part.at[pl.ds(first - base, last - first)]
                    off, count = first - start, last - first
                    to = pl.ds(s * block, block)
                    if f == 0:
                        copy(source, wq.at[pl.ds(off, count), to])
                    elif f == 1:
                        here = pl.multiple_of(core * wl_rows + off, 16)
                        copy(source, wl.at[pl.ds(here, count), to])
                    elif f == 2:
                        here = pl.multiple_of((index ^ s) * up_rows + off, 16)
                        copy(source, up.at[pl.ds(here, count)])
                    else:
                        copy(source, wo.at[pl.ds(off, count), to])
                start += size
            base += part.shape[0]
    for one in copies:
        one.start()
    for one in copies:
        one.wait()


def attend_kernel(at, *refs):
    sources, refs = refs[:13], refs[13:]
    (gain, cos, sin, mask, latent_gain, part_own, part_oth, normed_out, keys_out, queries_out, nope_out,
     probs_out, mixed_out, heads_out, unit_out, inverse_out, x, wq, wl, up, wo, sems) = refs
    assemble(at, sources, x, wq, wl, up, wo, sems)
    rows = x[...].astype(f32)
    normed = (rows * rms_stats(rows) * gain[...]).astype(bf16)
    normed_out[...] = normed
    query = mm_nt(normed, wq[...])
    latent_all = mm_nt(normed, wl[:R])
    inverse = rms_stats(latent_all)
    unit = latent_all * inverse
    unit_out[...] = unit
    inverse_out[...] = jnp.broadcast_to(inverse, inverse_out.shape)
    latent = (unit * latent_gain[...]).astype(bf16)
    key_rope = mm_nt(normed, jnp.concatenate([wl[R:], wl[R:]], axis=0))
    keys_out[:, :R] = latent
    keys_out[:, R:] = (key_rope * cos[...] + swap_quarters(key_rope) * sin[...]).astype(bf16)
    ropes = query[:, 2 * DN :]
    ropes = (ropes * cos[...] + swap_quarters(ropes) * sin[...]).astype(bf16)
    lane = lax.broadcasted_iota(jnp.int32, ropes.shape, 1)
    keys = keys_out[...]
    allowed = mask[...] > 0
    for h in range(2):
        nope = query[:, h * DN : (h + 1) * DN].astype(bf16)
        nope_out[:, h * DN : (h + 1) * DN] = nope
        queries_out[h, :, :R] = mm_nt(nope, up[:, h * (DN + DV) : h * (DN + DV) + DN]).astype(bf16)
        queries_out[h, :, R:] = jnp.where(lane // 64 == h, ropes, jnp.zeros_like(ropes))
        scores = mm_nt(queries_out[h], keys) * (DN + DR) ** (-0.5)
        scores = jnp.where(allowed, scores, masked_score)
        exps = jnp.exp(scores - jnp.max(scores, axis=1, keepdims=True))
        probs = exps / jnp.sum(exps, axis=1, keepdims=True)
        probs_out[h] = probs
        mixed = mm(probs.astype(bf16), latent).astype(bf16)
        mixed_out[h] = mixed
        heads_out[:, h * DV : (h + 1) * DV] = mm(
            mixed, up[:, h * (DN + DV) + DN : (h + 1) * (DN + DV)]
        ).astype(bf16)
    half = part_own.shape[1]
    part = mm(heads_out[...], wo[...]).astype(bf16)
    first = at[0] == 0
    part_own[...] = jnp.where(first, part[:, :half], part[:, half:])
    part_oth[...] = jnp.where(first, part[:, half:], part[:, :half])


def attend_back_kernel(at, *refs):
    sources, refs = refs[:13], refs[13:]
    (res, normed, cos, sin, latent_gain, keys, queries, nope, probs, mixed, heads, unit, inverse,
     back_own, back_oth, grad_wo, grad_wq, grad_wl, grad_wl_oth, grad_up, grad_gain, grad_latent_gain,
     gl_ref, gq_ref, gk_ref, x, wq, wl, up, wo, sems) = refs
    assemble(at, sources, x, wq, wl, up, wo, sems)
    res_rows = res[...]
    grad_wo[...] = mm_tn(heads[...], res_rows).astype(bf16)
    grad_heads = mm_nt(res_rows, wo[...]).astype(bf16)
    latent = keys[:, :R]
    lane = lax.broadcasted_iota(jnp.int32, cos.shape, 1)
    grad_ropes = jnp.zeros(cos.shape, f32)
    uw = DN + DV
    for h in range(2):
        grad_head = grad_heads[:, h * DV : (h + 1) * DV]
        up_key = up[:, h * uw : h * uw + DN]
        grad_mixed = mm_nt(grad_head, up[:, h * uw + DN : (h + 1) * uw]).astype(bf16)
        prob = probs[h]
        grad_att = mm_nt(grad_mixed, latent)
        delta = jnp.sum(prob * grad_att, axis=1, keepdims=True)
        score_grad = (prob * (grad_att - delta) * (DN + DR) ** (-0.5)).astype(bf16)
        grad_query = mm(score_grad, keys[...])
        grad_keys = mm_tn(score_grad, queries[h])
        grad_latent = grad_keys[:, :R] + mm_tn(prob.astype(bf16), grad_mixed)
        if h == 0:
            gk_ref[:, :R] = grad_latent
            gk_ref[:, R:] = grad_keys[:, R:]
        else:
            gk_ref[:, :R] += grad_latent
            gk_ref[:, R:] += grad_keys[:, R:]
        grad_ropes = grad_ropes + jnp.where(lane // 64 == h, grad_query[:, R:], 0.0)
        grad_ql = grad_query[:, :R].astype(bf16)
        gq_ref[:, h * DN : (h + 1) * DN] = mm(grad_ql, up_key).astype(bf16)
        grad_up[h * uw : h * uw + DN] = mm_tn(nope[:, h * DN : (h + 1) * DN], grad_ql).astype(bf16)
        grad_up[h * uw + DN : (h + 1) * uw] = mm_tn(grad_head, mixed[h]).astype(bf16)
    gq_ref[:, 2 * DN :] = (grad_ropes * cos[...] - swap_quarters(grad_ropes) * sin[...]).astype(bf16)
    grad_latent = gk_ref[:, :R]
    grad_latent_gain[...] = jnp.sum(grad_latent * unit[...], axis=0, keepdims=True)
    gl_ref[:, :R] = rms_back(grad_latent * latent_gain[...], unit[...], inverse[:, :1]).astype(bf16)
    key_ropes = gk_ref[:, R:]
    key_ropes = key_ropes + pltpu.roll(key_ropes, 64, 1)
    key_ropes = key_ropes * cos[...] - swap_quarters(key_ropes) * sin[...]
    gl_ref[:, R:] = key_ropes.astype(bf16)
    back = mm(gq_ref[...], wq[...]) + mm(gl_ref[:, :R], wl[:R]) + mm(gl_ref[:, R : R + DR], wl[R:])
    tree_rows = x[...].astype(f32)
    unit_rows = tree_rows * rms_stats(tree_rows)
    grad_gain[...] = jnp.sum(back * unit_rows, axis=0, keepdims=True)
    half = back_own.shape[1]
    back = back.astype(bf16)
    first = at[0] == 0
    back_own[...] = jnp.where(first, back[:, :half], back[:, half:])
    back_oth[...] = jnp.where(first, back[:, half:], back[:, :half])
    rows = normed[...]
    grad_wq[...] = mm_tn(gq_ref[...], rows).astype(bf16)
    cut = grad_wl.shape[0]
    low = mm_tn(gl_ref[:, : 3 * LANES], rows).astype(bf16)
    high = mm_tn(gl_ref[:, 2 * LANES :], rows).astype(bf16)
    low, high = low[:cut], high[cut - 2 * LANES : 2 * cut - 2 * LANES]
    grad_wl[...] = jnp.where(first, low, high)
    grad_wl_oth[...] = jnp.where(first, high, low)


def whole_call(kernel, sources, operands, outs, scratch, at, tree_len, wq_rows, wo_rows):
    scratch = scratch + [
        pltpu.VMEM((tree_len, D), bf16),
        pltpu.VMEM((wq_rows, D), bf16),
        pltpu.VMEM((R + DR, D), bf16),
        pltpu.VMEM((R, R), bf16),
        pltpu.VMEM((wo_rows, D), bf16),
        pltpu.SemaphoreType.DMA((32,)),
    ]
    return pl.pallas_call(
        kernel,
        in_specs=[pl.BlockSpec(memory_space=pltpu.SMEM)]
        + [pl.BlockSpec(memory_space=pl.ANY)] * len(sources)
        + [pl.BlockSpec(memory_space=pltpu.VMEM)] * len(operands),
        out_specs=[pl.BlockSpec(memory_space=pltpu.VMEM)] * len(outs),
        out_shape=[jax.ShapeDtypeStruct(shape, kind) for shape, kind in outs],
        scratch_shapes=scratch,
        compiler_params=pltpu.CompilerParams(vmem_limit_bytes=58 * 1024 * 1024),
        cost_estimate=pl.CostEstimate(flops=0, bytes_accessed=0, transcendentals=0),
    )(at, *sources, *operands)


def weight_kernel(segments, at, lefts, owns, others, out):
    c = pl.program_id(0)
    mine = (c // (pl.num_programs(0) // 2)) == at[0]

    def run(rights):
        to = 0
        for start, rows in segments:
            result = jnp.zeros((rows, out.shape[1]), f32)
            first = 0
            for right in rights:
                deep = right.shape[0]
                result = result + mm_tn(lefts[first : first + deep, start : start + rows], right[...])
                first += deep
            out[to : to + rows] = result.astype(bf16)
            to += rows

    @pl.when(mine)
    def _():
        run(owns)

    @pl.when(jnp.logical_not(mine))
    def _():
        run(others)


def weight_call(core, left, owns, others, segments, count):
    block = D // count
    rows = sum(size for first, size in segments)
    per_half = count // 2

    def body(at, *refs):
        parts = len(owns)
        weight_kernel(segments, at, refs[0], refs[1 : 1 + parts], refs[1 + parts : -1], refs[-1])

    columns = lambda c, at: (0, c % per_half)
    return pl.pallas_call(
        body,
        grid_spec=pltpu.PrefetchScalarGridSpec(
            num_scalar_prefetch=1,
            grid=(count,),
            in_specs=[pl.BlockSpec(left.shape, lambda c, at: (0, 0), pipeline_mode=pl.Buffered(1))]
            + [pl.BlockSpec((r.shape[0], block), columns) for r in owns + others],
            out_specs=pl.BlockSpec((rows, block), lambda c, at: (c, 0)),
        ),
        out_shape=jax.ShapeDtypeStruct((count * rows, block), bf16),
        compiler_params=pltpu.CompilerParams(
            dimension_semantics=("arbitrary",), vmem_limit_bytes=58 * 1024 * 1024
        ),
        cost_estimate=pl.CostEstimate(flops=0, bytes_accessed=0, transcendentals=0),
    )(jnp.reshape(core, (1,)).astype(jnp.int32), left, *owns, *others)


def per_device(
    layer_in,
    norm_gain,
    query_proj,
    latent_proj,
    latent_gain,
    latent_up,
    output_proj,
    ffn_gain,
    router,
    shared_gate,
    shared_up,
    shared_down,
    expert_gate,
    expert_up,
    expert_down,
    routes,
    leaf_parent,
    grad_out,
):
    tok = layer_in.shape[0]
    n_dp, n_ex = lax.axis_size("dp"), lax.axis_size("expert")
    i, j, core = lax.axis_index("dp"), lax.axis_index("expert"), lax.axis_index("tensor")
    tree_len = tok * n_ex
    seg_len = tree_len // 16
    trunk_len = 4 * seg_len
    block = D // n_dp
    sub = block // n_ex
    heads_local = output_proj.shape[0] // DV
    groups = min(n_ex, heads_local)
    hp = heads_local // groups
    qg = n_ex // groups
    group = j // qg
    n_q = n_ex // qg
    rows_q = tok * n_q
    qw = DN + DR
    uw = DN + DV
    score_scale = (DN + DR) ** (-0.5)

    x_rel = permute_blocks(layer_in, i, n_dp)
    gain_one = permute_blocks(norm_gain.astype(f32), i, n_dp)
    gain_two = permute_blocks(ffn_gain.astype(f32), i, n_dp)
    gain_latent = latent_gain.astype(f32)
    half = D // 2
    up_rows = R // n_dp
    by_kernel = qg == 1 and hp == 2 and tree_len <= 512 and n_ex == 4
    sh_width = shared_gate.shape[1] // (n_dp * n_ex)
    lanes = jnp.arange(LANES, dtype=jnp.int32) - sh_width
    route_lanes = jnp.any(routes[:, :, None] == lanes[None, None, :], axis=1).astype(bf16)

    def with_grad(which):
        return jnp.concatenate(
            [pick_half(x_rel, which, 1), pick_half(grad_out, which, 1), route_lanes], axis=1
        )

    xg_own, xg_other = with_grad(core), with_grad(1 - core)
    xg_got = gather_rel(xg_own, "expert")[1:]
    xg_there = [swap(p, "tensor", 1) for p in xg_got]
    grad_wide = half + LANES

    def grad_rows_of(got, own):
        return place_rows(
            [(p, 0, tok, k * tok, 0, (half, grad_wide)) for k, p in enumerate(got + [own])], tree_len
        )

    g_rows = grad_rows_of(xg_got, xg_own)
    wq_rows, wl_rows = hp * qw, (R + DR) // 2
    if by_kernel:
        at_pack = jnp.stack([group, core]).astype(jnp.int32)
        packed = pack_call(at_pack, query_proj, latent_proj.T, latent_up, output_proj, block)
        first = gather_parts(packed, xg_got)
        wl_parts = []
        for s, piece in enumerate(first):
            base = 0
            for part in piece:
                low = max(wq_rows, base)
                high = min(wq_rows + wl_rows, base + part.shape[0])
                if low < high:
                    wl_parts.append((part, low - base, high - low, low - wq_rows, s * block))
                base += part.shape[0]
        wl_there = swap(place_rows(wl_parts, wl_rows), "tensor", 1)
        gathered = [x_rel] + xg_got + xg_there + [wl_there] + [p for piece in first for p in piece]
        ready = first[3]
    else:
        wq_own = lax.dynamic_slice_in_dim(query_proj, group * hp * qw, hp * qw, 1).T
        wl_own = pick_half(latent_proj.T, core, 0)
        up_own = lax.dynamic_slice_in_dim(latent_up, group * hp * uw, hp * uw, 1)
        wo_own = lax.dynamic_slice_in_dim(output_proj, group * hp * DV, hp * DV, 0)
        x_got = jnp.concatenate([p[:, :half] for p in xg_got], axis=0)
        x_there = jnp.concatenate([p[:, :half] for p in xg_there], axis=0)
        wq = jnp.concatenate(gather_dp(wq_own), axis=1)
        wl_got = jnp.concatenate(gather_dp(wl_own), axis=1)
        wl = rows_join(wl_got, swap(wl_got, "tensor", 1), core)
        up = jnp.concatenate(canonical(gather_rel(up_own, "dp"), i), axis=0)
        wo = jnp.concatenate(gather_rel(wo_own, "dp"), axis=1)
        x_tree = jnp.concatenate([x_rel, halves(x_got, x_there, core, 1)], axis=0)
        ready = [wq, wo]

    local_experts = expert_gate.shape[0]
    parts = n_dp // local_experts
    width = expert_gate.shape[2] // parts
    chosen, part_at = i // parts, (i % parts) * width
    expert_id = j * local_experts + chosen
    sh_sent = []
    for c in range(n_dp):
        at_unit = (j * n_dp + c) * sh_width
        sh_sent += [
            lax.dynamic_slice_in_dim(shared_gate, at_unit, sh_width, 1).T,
            lax.dynamic_slice_in_dim(shared_up, at_unit, sh_width, 1).T,
            lax.dynamic_slice_in_dim(shared_down, at_unit, sh_width, 0),
        ]
    sh_sent = order([jnp.concatenate(sh_sent, axis=0)], ready)[0]
    sh_got = lax.all_to_all(sh_sent, "dp", 0, 0, tiled=True)
    sh_rows = jnp.concatenate(
        [sh_got[c * 3 * sh_width : (c + 1) * 3 * sh_width] for c in range(n_dp)], axis=1
    )
    hidden_width = -(-(LANES + width) // LANES) * LANES

    room = LANES - sh_width
    shared_w = jnp.concatenate(
        [
            jnp.pad(sh_rows[:sh_width], ((0, room), (0, 0))),
            sh_rows[sh_width : 2 * sh_width],
            router.T,
            jnp.zeros((room - EXPERTS, D), bf16),
            jnp.pad(sh_rows[2 * sh_width :], ((0, room), (0, 0))),
        ],
        axis=0,
    )
    feed_weights = [jnp.swapaxes(expert_gate, 1, 2), jnp.swapaxes(expert_up, 1, 2), expert_down]
    pick = chosen
    if parts > 1:
        feed_weights = [lax.dynamic_slice(w, (chosen, part_at, 0), (1, width, D)) for w in feed_weights]
        pick = chosen * 0
    feed_weights = feed_weights + [shared_w]

    slots = jnp.arange(tree_len, dtype=jnp.int32)
    token_index = (j ^ (slots // tok)) * tok + slots % tok

    def queries_of(values):
        if qg == 1:
            return values
        split = values.reshape((n_q, qg, tok) + values.shape[1:])[:, 0]
        return split.reshape((rows_q,) + values.shape[1:])

    position, segment, parent, grand = tree_layout(leaf_parent, token_index, trunk_len, seg_len)
    freqs = 10000.0 ** (-2.0 * jnp.arange(DR // 2, dtype=f32) / DR)
    angles = position.astype(f32)[:, None] * freqs[None, :]
    cosine, sine = jnp.cos(angles), jnp.sin(angles)
    q_cos, q_sin = queries_of(cosine), queries_of(sine)
    allowed = visible(
        queries_of(segment),
        queries_of(parent),
        queries_of(grand),
        queries_of(token_index),
        segment,
        token_index,
    )

    own_rows = x_rel.astype(f32)
    inverse_one = rms_stats(own_rows)
    unit_one = own_rows * inverse_one
    at_all = jnp.stack([core, i]).astype(jnp.int32)
    if by_kernel:
        cos_lanes = jnp.concatenate([cosine] * 4, axis=1)
        sin_lanes = jnp.concatenate([-sine, sine] * 2, axis=1)
        rows, wide = tree_len, (tree_len, LANES)
        (
            part_own, part_other, normed, keys, queries, nope, probs, mixed, heads_out, unit_latent,
            inverse_latent,
        ) = whole_call(
            attend_kernel,
            gathered,
            [
                gain_one[None], cos_lanes, sin_lanes, allowed.astype(bf16),
                gain_latent[None],
            ],
            [
                ((rows, half), bf16), ((rows, half), bf16),
                ((rows, D), bf16), ((rows, R + LANES), bf16), ((2, rows, R + LANES), bf16),
                ((rows, 2 * DN), bf16), ((2, rows, rows), f32), ((2, rows, R), bf16),
                ((rows, 2 * DV), bf16), ((rows, R), f32), (wide, f32),
            ],
            [],
            at_all, tree_len, wq_rows, hp * DV,
        )
        part_other = order([part_other], [sh_got])[0]
    else:
        tree_unit = x_tree.astype(f32)
        tree_unit = tree_unit * rms_stats(tree_unit)
        normed = (tree_unit * gain_one).astype(bf16)
        normed_q = queries_of(normed)
        query_all = mm_nt(normed_q, wq)
        latent_all = mm_nt(normed, wl)
        inverse_latent = rms_stats(latent_all[:, :R])
        unit_latent = latent_all[:, :R] * inverse_latent
        latent = (unit_latent * gain_latent).astype(bf16)
        key_rope = rotate(latent_all[:, R:], cosine, sine).astype(bf16)
        keys = jnp.concatenate([latent, key_rope], axis=1)
        up_key = [up[:, h * uw : h * uw + DN] for h in range(hp)]
        up_value = [up[:, h * uw + DN : (h + 1) * uw] for h in range(hp)]
        query_nope = [query_all[:, h * qw : h * qw + DN].astype(bf16) for h in range(hp)]
        queries = jnp.concatenate(
            [
                jnp.concatenate(
                    [
                        mm_nt(query_nope[h], up_key[h]).astype(bf16),
                        rotate(query_all[:, h * qw + DN : (h + 1) * qw], q_cos, q_sin).astype(bf16),
                    ],
                    axis=1,
                )
                for h in range(hp)
            ],
            axis=0,
        )
        raw_scores = mm_nt(queries, keys).reshape(hp, rows_q, tree_len)
        scores = jnp.where(allowed[None], raw_scores * score_scale, masked_score)
        exp_scores = jnp.exp(scores - jnp.max(scores, axis=-1, keepdims=True))
        probs = exp_scores / jnp.sum(exp_scores, axis=-1, keepdims=True)
        probs = probs.reshape(hp * rows_q, tree_len)
        probs_low = probs.astype(bf16)
        mixed = mm(probs_low, latent).astype(bf16)
        mixed_head = [mixed[h * rows_q : (h + 1) * rows_q] for h in range(hp)]
        heads_out = jnp.concatenate(
            [mm(mixed_head[h], up_value[h]).astype(bf16) for h in range(hp)], axis=1
        )
        part_own, part_other = mm(heads_out, pick_half(wo, core, 1)), mm(
            heads_out, pick_half(wo, 1 - core, 1)
        )

    g_parts = gather_parts(g_rows)

    def tree_scatter(partial_own, partial_other, count, stride, before=None):
        there = swap(partial_other.astype(bf16), "tensor", 1)
        joined = (partial_own.astype(f32) + there.astype(f32)).astype(bf16)
        own = total(
            exchange_rel(
                [joined[s * tok : (s + 1) * tok] for s in range(count)], "expert", stride
            )
        )
        if before is not None:
            own = order([own], before)[0]
        return halves(own, swap(own, "tensor", 1), core, 1)

    attention = tree_scatter(part_own, part_other, n_q, qg, g_parts[1] + g_parts[2])
    residual = own_rows + attention
    inverse_two = rms_stats(residual)
    unit_two = residual * inverse_two
    normed_two = permute_blocks((unit_two * gain_two).astype(bf16), i, n_dp)

    n_half = pick_half(normed_two, core, 1)
    n_other = pick_half(normed_two, 1 - core, 1)
    n_others = join_rows(gather_rel(n_half, "expert")[1:])
    own_parts = gather_parts(n_half)
    n_others = order([n_others], g_parts[3] + own_parts[1] + own_parts[2])[0]
    n_there = swap(n_others, "tensor", 1)
    g_rest = join_rows(g_parts[1] + g_parts[2] + g_parts[3])
    grad_own = [g_rows, g_rest]
    grad_other = [grad_rows_of(xg_there, xg_other), swap(g_rest, "tensor", 1)]
    at = jnp.stack([pick, core, sh_width + expert_id]).astype(jnp.int32)
    tree_rows = n_others.shape[0] + tok
    tokens = tree_rows * n_dp

    def feed(k, own, other, kept, others):
        return feed_call(
            at, sh_width, width, hidden_width, own, other, grad_own[k], grad_other[k],
            feed_weights, (k * tree_rows, tokens), kept, others,
        )

    rows_own = [join_rows([n_others, n_half])]
    rows_other = [join_rows([n_there, n_other])]
    made = feed(0, rows_own[0], rows_other[0], [], [])
    other_parts = gather_parts(n_others, [made[0]])
    near = join_rows(
        other_parts[1] + own_parts[1] + other_parts[2] + own_parts[2], [made[0]]
    )
    far = join_rows(other_parts[3] + own_parts[3])
    rows_own.append(join_rows([near, far]))
    rows_other.append(join_rows([swap(near, "tensor", 1), swap(far, "tensor", 1)]))
    grad_parts, out_parts = [made[2:4]], [made[4:6]]
    theirs = [swap(made[3], "tensor", 1)]
    out_there = [swap(made[5], "tensor", 1)]
    made = feed(1, rows_own[1], rows_other[1], list(made[:2]), theirs + out_there)
    grad_parts.append(made[2:4])
    out_parts.append(made[4:6])
    hidden_scaled, back_pre = made[:2]

    def join(mine, theirs):
        return (mine.astype(f32) + swap(theirs, "tensor", 1).astype(f32)).astype(bf16)

    routed_at, up_at = (LANES, width), (hidden_width + LANES, width)
    sent_width = -(-sh_width // 16) * 16
    sent_router = -(-(sh_width + EXPERTS) // 16) * 16

    theirs.append(swap(grad_parts[1][1], "tensor", 1))
    many = tree_rows - tok

    def joined(mine, there, low, high):
        return (mine[low:high].astype(f32) + there[low:high].astype(f32)).astype(bf16)

    def cut_of(parts, there, low, high):
        return [joined(parts[0], there[0], low, high)] + [
            joined(parts[1], there[1], s * tree_rows + low, s * tree_rows + high)
            for s in range(n_dp - 1)
        ]

    grad_mine = [p[0] for p in grad_parts]
    hidden_late = order([hidden_scaled], [theirs[1]])[0]
    down_sent = weight_call(
        core, hidden_late, grad_own, grad_other, [routed_at, (0, sent_width)], n_dp
    )
    others_state = reduce_first(cut_of(grad_mine, theirs, 0, many))
    others_first = list(others_state[2:])
    back_late = order([back_pre], others_first)[0]
    gate_sent = weight_call(
        core, back_late, rows_own, rows_other,
        [routed_at, (0, sent_width), (hidden_width, sent_router)], n_dp,
    )
    own_state = reduce_first(order(cut_of(grad_mine, theirs, many, tree_rows), others_first))
    gn2_others = reduce_second(others_state, [down_sent])
    gn2_own = order([reduce_second(own_state)], [gate_sent])[0]

    out_there.append(swap(order([out_parts[1][1]], [theirs[1]])[0], "tensor", 1))
    out_state = reduce_first(
        order(
            cut_of(
                [p[0] for p in out_parts],
                out_there,
                0,
                tree_rows,
            ),
            [gn2_own],
        )
    )
    out_first = list(out_state[2:])
    z_sent = gn2_others
    z_got = exchange_rel(
        [gn2_own] + [z_sent[s * tok : (s + 1) * tok] for s in range(n_ex - 1)], "expert"
    )
    back_last = order([back_late], [gn2_others])[0]
    up_sent = weight_call(core, back_last, rows_own, rows_other, [up_at], n_dp)
    gn2_half = order([total(z_got)], [up_sent])[0]
    gn2 = permute_blocks(halves(gn2_half, swap(gn2_half, "tensor", 1), core, 1), i, n_dp)

    grad_ffn_gain = jnp.sum(gn2 * unit_two, axis=0, keepdims=True)
    grad_residual = permute_blocks(grad_out, i, n_dp).astype(f32) + rms_back(
        gn2 * gain_two, unit_two, inverse_two
    )
    res_half = pick_half(grad_residual.astype(bf16), core, 1)

    out_mine = reduce_second(out_state)

    def to_owners(sent, others):
        sent = order([sent], others)[0]
        return lax.all_to_all(sent, "dp", 0, 0, tiled=True).reshape(n_dp, -1, block)

    down_got = to_owners(down_sent, [gn2_own])
    gate_got = to_owners(gate_sent, [gn2_half])
    up_got = to_owners(up_sent, [gn2_half])
    router_at = width + sent_width + sh_width
    router_block = gate_sent.reshape(n_dp, -1, block)[:, router_at : router_at + EXPERTS]
    grad_router_rows = jnp.concatenate(
        [lax.dynamic_index_in_dim(router_block, i ^ s, 0, False) for s in range(n_dp)], axis=1
    )

    res_others = gather_z(res_half)
    res_others = halves(res_others, swap(res_others, "tensor", 1), core, 1)
    res_tree = jnp.concatenate([grad_residual.astype(bf16), res_others], axis=0)
    res_tree = order([res_tree], out_first)[0]
    if by_kernel:
        (
            back_mine, back_other, grad_wo, wq_grad, wl_grad, wl_sent, by_r, grad_norm_gain,
            grad_latent_gain,
        ) = (
            whole_call(
                attend_back_kernel,
                gathered,
                [
                    res_tree, normed, cos_lanes, sin_lanes, gain_latent[None], keys, queries, nope,
                    probs, mixed, heads_out, unit_latent, inverse_latent,
                ],
                [
                    ((rows, half), bf16), ((rows, half), bf16), ((2 * DV, D), bf16),
                    ((2 * qw, D), bf16), ((wl_rows, D), bf16), ((wl_rows, D), bf16),
                    ((2 * uw, R), bf16), ((1, D), f32),
                    ((1, R), f32),
                ],
                [
                    pltpu.VMEM((rows, R + LANES), bf16),
                    pltpu.VMEM((rows, 2 * qw), bf16),
                    pltpu.VMEM((rows, R + LANES), f32),
                ],
                at_all, tree_len, wq_rows, hp * DV,
            )
        )
    else:
        res_q = res_tree
        res_q = queries_of(res_q)
        grad_heads = mm_nt(res_q, wo).astype(bf16)
        grad_head = [grad_heads[:, h * DV : (h + 1) * DV] for h in range(hp)]

        grad_wo = mm_tn(heads_out, res_q)

        grad_mixed = jnp.concatenate(
            [mm_nt(grad_head[h], up_value[h]).astype(bf16) for h in range(hp)], axis=0
        )
        grad_att = mm_nt(grad_mixed, latent)
        delta = jnp.sum(probs * grad_att, axis=-1, keepdims=True)
        score_grad = (probs * (grad_att - delta) * score_scale).astype(bf16)
        grad_queries = mm(score_grad, keys)
        grad_keys = mm_tn(score_grad, queries)
        grad_latent_keys = grad_keys[:, :R] + mm_tn(probs_low, grad_mixed)
        grad_query_latent = grad_queries[:, :R].astype(bf16)
        grad_query_parts, grad_up_parts = [], []
        for h in range(hp):
            rows = slice(h * rows_q, (h + 1) * rows_q)
            grad_query_parts.append(mm(grad_query_latent[rows], up_key[h]))
            grad_query_parts.append(rotate_back(grad_queries[rows, R:], q_cos, q_sin))
            grad_up_parts.append(mm_tn(query_nope[h], grad_query_latent[rows]))
            grad_up_parts.append(mm_tn(grad_head[h], mixed_head[h]))
        grad_query_all = jnp.concatenate(grad_query_parts, axis=1).astype(bf16)
        grad_latent_gain = jnp.sum(grad_latent_keys * unit_latent, axis=0, keepdims=True)
        grad_latent_all = jnp.concatenate(
            [
                rms_back(grad_latent_keys * gain_latent, unit_latent, inverse_latent),
                rotate_back(grad_keys[:, R:], cosine, sine),
            ],
            axis=1,
        ).astype(bf16)

        grad_query_rows = grad_query_all
        if qg > 1:
            grad_query_rows = jnp.pad(
                grad_query_all.reshape(n_q, 1, tok, -1), ((0, 0), (0, qg - 1), (0, 0), (0, 0))
            ).reshape(tree_len, -1)
        def back_half(which):
            return mm(grad_query_rows, pick_half(wq, which, 1)) + mm(
                grad_latent_all, pick_half(wl, which, 1)
            )

        back_mine, back_other = back_half(core), back_half(1 - core)
        norm_mine = jnp.sum(back_mine * pick_half(tree_unit, core, 1), axis=0, keepdims=True)
        norm_other = jnp.sum(back_other * pick_half(tree_unit, 1 - core, 1), axis=0, keepdims=True)
        grad_norm_gain = halves(norm_mine, norm_other, core, 1)
        wq_grad, wl_grad = mm_tn(grad_query_all, normed_q), mm_tn(grad_latent_all, normed)
        by_r = jnp.concatenate(grad_up_parts, axis=0)


    up_sub = up_rows // n_ex
    gain_row = jnp.concatenate(
        [
            lax.dynamic_slice_in_dim(grad_latent_gain, (i ^ s) * up_rows, up_rows, 1)
            for s in range(n_dp)
        ],
        axis=1,
    ).reshape(n_dp * n_ex, up_sub)
    gain_row = jnp.pad(gain_row, ((0, 0), (0, sub - up_sub))).reshape(1, D)
    if not by_kernel:
        wl_grad = wl_grad.astype(bf16)
        wl_grad, wl_sent = pick_half(wl_grad, core, 0), pick_half(wl_grad, 1 - core, 0)
    wl_there = swap(wl_sent, "tensor", 1)
    wl_grad = wl_grad.astype(f32) + wl_there.astype(f32)
    small_rows = jnp.concatenate(
        [
            grad_norm_gain,
            0.5 * grad_ffn_gain,
            grad_router_rows.astype(f32),
            gain_row,
            jnp.zeros((13, D), f32),
        ],
        axis=0,
    )
    by_d = [grad_wo, wq_grad, wl_grad, small_rows]
    by_r = by_r.astype(bf16)
    d_rows, r_rows = sum(p.shape[0] for p in by_d), by_r.shape[0]
    by_r = [lax.dynamic_slice_in_dim(by_r, (i ^ s) * up_rows, up_rows, 1) for s in range(n_dp)]
    split_r = block // up_rows
    cut_r = r_rows // split_r
    by_r = jnp.concatenate(
        [
            jnp.concatenate([by_r[s][c * cut_r : (c + 1) * cut_r] for c in range(split_r)], 1)
            for s in range(n_dp)
        ],
        axis=1,
    )
    by_d[0] = order([by_d[0]], [down_got])[0]
    tail_state = reduce_first(stack_rows(by_d + [by_r], block))
    grad_normed = tree_scatter(back_mine, back_other, n_ex, 1, list(tail_state[2:]))
    grad_in = permute_blocks(
        grad_residual + rms_back(grad_normed * gain_one, unit_one, inverse_one), i, n_dp
    )

    mine = reduce_second(tail_state, [gate_got])
    out_mine = order([out_mine], [back_mine])[0]
    ffn_half = along_z(out_mine[:many], out_mine[many:])
    out_half = (pick_half(permute_blocks(residual, i, n_dp), core, 1) + ffn_half).astype(bf16)
    layer_out = halves(out_half, swap(out_half, "tensor", 1), core, 1)

    mine_r = jnp.concatenate(
        [mine[d_rows:, c * up_rows : (c + 1) * up_rows] for c in range(split_r)], axis=0
    )

    def z_piece(s):
        to = j ^ s
        rows_r = lax.dynamic_slice_in_dim(mine_r, to * up_sub, up_sub, 1)
        cut = r_rows * up_sub // sub
        return jnp.concatenate(
            [lax.dynamic_slice_in_dim(mine[:d_rows], to * sub, sub, 1)]
            + [
                jnp.concatenate(
                    [rows_r[c * cut : (c + 1) * cut] for c in range(sub // up_sub)], axis=1
                )
            ],
            axis=0,
        )

    got = exchange_rel([z_piece(s) for s in range(n_ex)], "expert")

    def over_groups(pieces):
        ordered = canonical(pieces, j)
        return jnp.concatenate(
            [total(ordered[g * qg : (g + 1) * qg]) for g in range(groups)], axis=0
        )

    ends = [hp * DV, hp * DV + wq_rows, hp * DV + wq_rows + wl_rows]
    grad_output_proj = over_groups([p[: ends[0]] for p in got])
    grad_query_rows = [p[ends[0] : ends[1]] for p in got]
    if by_kernel:
        grad_query_rows = [
            jnp.concatenate(
                [p[:DN], p[2 * DN : 2 * DN + DR], p[DN : 2 * DN], p[2 * DN + DR :]], axis=0
            )
            for p in grad_query_rows
        ]
    grad_query_proj = over_groups(grad_query_rows).T
    grad_latent_up = over_groups(
        [
            jnp.concatenate(
                [p[d_rows:, c * up_sub : (c + 1) * up_sub] for c in range(sub // up_sub)], axis=0
            )
            for p in got
        ]
    ).T
    rest = total([p[ends[1] : d_rows] for p in got])
    rest_there = swap(rest, "tensor", 1)
    grad_latent_proj = rows_join(rest[:wl_rows], rest_there[:wl_rows], core).T
    small = rest[wl_rows:] + rest_there[wl_rows:]

    down_got, gate_got = order([down_got, gate_got], list(tail_state[2:]))
    up_got = order([up_got], [mine])[0]
    shared_all = jnp.concatenate(
        [gate_got[:, width : width + 2 * sent_width], down_got[:, width:]], axis=1
    )
    shared_all = jnp.stack(
        canonical(
            exchange_rel(
                [lax.dynamic_slice_in_dim(shared_all, (j ^ s) * sub, sub, 2) for s in range(n_ex)],
                "expert",
            ),
            j,
        )
    )

    def shared_part(k):
        rows = shared_all[:, :, k * sent_width : k * sent_width + sh_width]
        return rows.reshape(-1, sub).astype(f32)

    def expert_part(got):
        return got[:, :width].reshape(local_experts, parts * width, block).astype(f32)

    grad_shared_gate, grad_shared_up = shared_part(0).T, shared_part(1).T
    grad_shared_down = shared_part(2)
    grad_expert_gate = jnp.swapaxes(expert_part(gate_got), 1, 2)
    grad_expert_up = jnp.swapaxes(expert_part(up_got), 1, 2)
    grad_expert_down = expert_part(down_got)

    return (
        layer_out,
        grad_in,
        small[0],
        grad_query_proj,
        grad_latent_proj,
        small[2 + EXPERTS, :up_sub],
        grad_latent_up,
        grad_output_proj,
        small[1],
        small[2 : 2 + EXPERTS].T,
        grad_shared_gate,
        grad_shared_up,
        grad_shared_down,
        grad_expert_gate,
        grad_expert_up,
        grad_expert_down,
    )


def solution(mesh):
    placed = (
        P(("dp", "expert"), None),
        P(),
        P("dp", "tensor"),
        P("dp", None),
        P(),
        P("dp", "tensor"),
        P("tensor", "dp"),
        P(),
        P(),
        P("dp", "tensor"),
        P("dp", "tensor"),
        P("tensor", "dp"),
        P("expert", None, "tensor"),
        P("expert", None, "tensor"),
        P("expert", "tensor", None),
        P(("dp", "expert"), None),
        P(),
        P(("dp", "expert"), None),
    )
    return jax.shard_map(
        per_device,
        mesh=mesh,
        in_specs=placed,
        out_specs=(
            P(("dp", "expert"), None),
            P(("dp", "expert"), None),
            P(("dp", "expert")),
            P(("dp", "expert"), "tensor"),
            P(("dp", "expert"), None),
            P(("dp", "expert")),
            P(("dp", "expert"), "tensor"),
            P("tensor", ("dp", "expert")),
            P(("dp", "expert")),
            P(("dp", "expert"), None),
            P(("dp", "expert"), "tensor"),
            P(("dp", "expert"), "tensor"),
            P("tensor", ("dp", "expert")),
            P("expert", "dp", "tensor"),
            P("expert", "dp", "tensor"),
            P("expert", "tensor", "dp"),
        ),
        check_vma=False,
    )
```

```python
import functools

import jax
import jax.numpy as jnp
from jax import lax
from jax.experimental import pallas as pl
from jax.experimental.pallas import tpu as pltpu
from jax.sharding import PartitionSpec as P

D = 2048
DN = 128
DR = 64
DV = 128
R = 512
EXPERTS = 16
NB = 4
NL = 2
LANES = 128

epsilon = 1e-06
masked_score = -1e30
bf16 = jnp.bfloat16
f32 = jnp.float32


def mm(left, right):
    return jnp.dot(left, right, preferred_element_type=f32)


def mm_nt(left, right):
    return lax.dot_general(left, right, (((1,), (1,)), ((), ())), preferred_element_type=f32)


def mm_tn(left, right):
    return lax.dot_general(left, right, (((0,), (0,)), ((), ())), preferred_element_type=f32)


def rms_stats(values):
    return lax.rsqrt(jnp.mean(values * values, axis=-1, keepdims=True) + epsilon)


def rms_back(grad_normed, unit_rows, inverse):
    return inverse * (
        grad_normed - unit_rows * jnp.mean(grad_normed * unit_rows, axis=-1, keepdims=True)
    )


def rotate(values, cosine, sine):
    half_width = values.shape[-1] // 2
    first_half = values[..., :half_width]
    second_half = values[..., half_width:]
    return jnp.concatenate(
        [first_half * cosine - second_half * sine, second_half * cosine + first_half * sine],
        axis=-1,
    )


def rotate_back(grads_in, cosine, sine):
    half_width = grads_in.shape[-1] // 2
    first_half = grads_in[..., :half_width]
    second_half = grads_in[..., half_width:]
    return jnp.concatenate(
        [first_half * cosine + second_half * sine, second_half * cosine - first_half * sine],
        axis=-1,
    )


def tree_layout(leaf_parent, token_index, trunk_len, seg_len):
    beyond = token_index - trunk_len
    in_trunk = token_index < trunk_len
    in_branch = (beyond >= 0) & (beyond < NB * seg_len)
    in_leaf = beyond >= NB * seg_len
    leaf_offset = beyond - NB * seg_len
    leaf_index = jnp.clip(leaf_offset // seg_len, 0, NB * NL - 1)
    position = jnp.where(
        in_trunk,
        token_index,
        jnp.where(
            in_branch, trunk_len + beyond % seg_len, trunk_len + seg_len + leaf_offset % seg_len
        ),
    )
    segment = jnp.where(
        in_trunk, 0, jnp.where(in_branch, 1 + beyond // seg_len, 1 + NB + leaf_index)
    )
    leaf_match = (leaf_index[:, None] == jnp.arange(NB * NL, dtype=jnp.int32)[None, :]).astype(
        jnp.int32
    )
    branch_of_leaf = 1 + jnp.sum(leaf_match * leaf_parent[None, :], axis=1)
    parent = jnp.where(in_trunk, -1, jnp.where(in_branch, 0, branch_of_leaf))
    grand = jnp.where(in_leaf, 0, -1)
    return (position, segment, parent, grand.astype(jnp.int32))


def visible(query_segment, query_parent, query_grand, query_index, key_segment, key_index):
    same_segment = (query_segment[:, None] == key_segment[None, :]) & (
        key_index[None, :] <= query_index[:, None]
    )
    ancestor = (key_segment[None, :] == query_parent[:, None]) | (
        key_segment[None, :] == query_grand[:, None]
    )
    return same_segment | ancestor


def swap(values, axis, step):
    return lax.ppermute(values, axis, [(k, k ^ step) for k in range(lax.axis_size(axis))])


def gather_rel(values, axis):
    size = lax.axis_size(axis)
    if size <= 4:
        return [values] + [swap(values, axis, s) for s in range(1, size)]
    full = lax.all_gather(values, axis)
    me = lax.axis_index(axis)
    return [lax.dynamic_index_in_dim(full, me ^ s, 0, False) for s in range(size)]


def exchange_rel(pieces, axis, stride=1):
    size = lax.axis_size(axis)
    if size <= 4:
        return [pieces[0]] + [swap(p, axis, k * stride) for k, p in enumerate(pieces) if k]
    me = lax.axis_index(axis)
    zero = jnp.zeros_like(pieces[0])
    full = jnp.stack([pieces[s // stride] if s % stride == 0 else zero for s in range(size)])
    order = me ^ jnp.arange(size)
    sent = lax.all_to_all(jnp.take(full, order, axis=0), axis, 0, 0, tiled=True)
    back = jnp.take(sent, order, axis=0)
    return [back[k * stride] for k in range(len(pieces))]


def canonical(pieces, me):
    stacked = jnp.stack(pieces)
    return [lax.dynamic_index_in_dim(stacked, me ^ c, 0, False) for c in range(len(pieces))]


def permute_blocks(values, me, count):
    width = values.shape[-1] // count
    return jnp.concatenate(
        [
            lax.dynamic_slice_in_dim(values, (me ^ s) * width, width, values.ndim - 1)
            for s in range(count)
        ],
        axis=-1,
    )


def total(pieces):
    result = pieces[0].astype(f32)
    for piece in pieces[1:]:
        result = result + piece.astype(f32)
    return result


def halves(own, other, core, dim):
    return jnp.where(
        core == 0,
        jnp.concatenate([own, other], axis=dim),
        jnp.concatenate([other, own], axis=dim),
    )


def pick_half(values, which, dim):
    width = values.shape[dim] // 2
    return lax.dynamic_slice_in_dim(values, which * width, width, dim)


def gather_shared(values, axis, core, dim):
    mine = gather_rel(pick_half(values, core, dim), axis)
    return [values] + [halves(p, swap(p, "tensor", 1), core, dim) for p in mine[1:]]


def keep_kernel(*refs):
    pass


def order(values, others):
    count, total_count = len(values), len(values) + len(others)
    anywhere = pl.BlockSpec(memory_space=pl.ANY)
    return pl.pallas_call(
        keep_kernel,
        in_specs=[anywhere] * total_count,
        out_specs=[anywhere] * count,
        out_shape=[jax.ShapeDtypeStruct(v.shape, v.dtype) for v in values],
        input_output_aliases={k: k for k in range(count)},
        cost_estimate=pl.CostEstimate(flops=0, bytes_accessed=0, transcendentals=0),
    )(*values, *others)


def place_rows(parts, rows, others=()):
    spans = [p[5] if len(p) > 5 else (0, p[0].shape[1]) for p in parts]
    columns = max(part[4] + span[1] for part, span in zip(parts, spans))

    def body(*refs):
        out, sems = refs[-2], refs[-1]
        copies = []
        for k, part in enumerate(parts):
            source = refs[k].at[pl.ds(part[1], part[2]), pl.ds(*spans[k])]
            target = out.at[pl.ds(part[3], part[2]), pl.ds(part[4], spans[k][1])]
            copies.append(pltpu.make_async_copy(source, target, sems.at[k]))
        for copy in copies:
            copy.start()
        for copy in copies:
            copy.wait()

    anywhere = pl.BlockSpec(memory_space=pl.ANY)
    return pl.pallas_call(
        body,
        in_specs=[anywhere] * (len(parts) + len(others)),
        out_specs=pl.BlockSpec(memory_space=pltpu.VMEM),
        out_shape=jax.ShapeDtypeStruct((rows, columns), parts[0][0].dtype),
        scratch_shapes=[pltpu.SemaphoreType.DMA((len(parts),))],
        compiler_params=pltpu.CompilerParams(vmem_limit_bytes=48 * 1024 * 1024),
        cost_estimate=pl.CostEstimate(flops=0, bytes_accessed=0, transcendentals=0),
    )(*[part[0] for part in parts], *others)


def pack_kernel(at, query, latent, up, out_w, packed):
    turned = query[...].T
    rows = DN + DR
    packed[0:DN] = turned[:DN]
    packed[DN : 2 * DN] = turned[rows : rows + DN]
    packed[2 * DN : 2 * DN + DR] = turned[DN:rows]
    packed[2 * DN + DR : 2 * rows] = turned[rows + DN :]
    first = 2 * rows
    for ref in (latent, up, out_w):
        packed[first : first + ref.shape[0]] = ref[...]
        first += ref.shape[0]


def pack_call(at, query_proj, latent_t, latent_up, output_proj, wide):
    block = query_proj.shape[0]
    qw, uw = 2 * (DN + DR), 2 * (DN + DV)
    sizes = [qw, latent_t.shape[0] // 2, latent_up.shape[0], 2 * DV]
    return pl.pallas_call(
        pack_kernel,
        grid_spec=pltpu.PrefetchScalarGridSpec(
            num_scalar_prefetch=1,
            grid=(1,),
            in_specs=[
                pl.BlockSpec((block, qw), lambda m, at: (0, at[0])),
                pl.BlockSpec((sizes[1], block), lambda m, at: (at[1], 0)),
                pl.BlockSpec((sizes[2], uw), lambda m, at: (0, at[0])),
                pl.BlockSpec((sizes[3], block), lambda m, at: (at[0], 0)),
            ],
            out_specs=pl.BlockSpec((sum(sizes), block), lambda m, at: (0, 0)),
        ),
        out_shape=jax.ShapeDtypeStruct((sum(sizes), block), bf16),
        compiler_params=pltpu.CompilerParams(vmem_limit_bytes=24 * 1024 * 1024),
        cost_estimate=pl.CostEstimate(flops=0, bytes_accessed=0, transcendentals=0),
    )(at, query_proj, latent_t, latent_up, output_proj)


def join_rows(arrays, others=()):
    parts, at = [], 0
    for array in arrays:
        parts.append((array, 0, array.shape[0], at, 0))
        at += array.shape[0]
    return place_rows(parts, at, others)


def gather_parts(values, between=None):
    if lax.axis_size("dp") != 4:
        return [[p] for p in gather_rel(values, "dp")]
    cut = values.shape[0] // 2
    first, second = swap(values, "dp", 1), swap(values, "dp", 2)
    low, high = first[:cut], second[cut:]
    if between is not None:
        low, high = order([low, high], between)
    return [[values], [first], [second], [swap(low, "dp", 2), swap(high, "dp", 1)]]


def gather_dp(values, between=None):
    return [p[0] if len(p) == 1 else join_rows(p) for p in gather_parts(values, between)]


def stack_kernel(*refs):
    at = 0
    for ref in refs[:-1]:
        refs[-1][at : at + ref.shape[0]] = ref[...].astype(bf16)
        at += ref.shape[0]


def stack_rows(parts, block):
    rows, columns = sum(p.shape[0] for p in parts), parts[0].shape[1]
    made = pl.pallas_call(
        stack_kernel,
        grid=(columns // block,),
        in_specs=[pl.BlockSpec((p.shape[0], block), lambda c: (0, c)) for p in parts],
        out_specs=pl.BlockSpec((rows, block), lambda c: (c, 0)),
        out_shape=jax.ShapeDtypeStruct((rows * (columns // block), block), bf16),
        compiler_params=pltpu.CompilerParams(vmem_limit_bytes=32 * 1024 * 1024),
        cost_estimate=pl.CostEstimate(flops=0, bytes_accessed=8 * rows * columns, transcendentals=0),
    )(*parts)
    return [made[c * rows : (c + 1) * rows] for c in range(columns // block)]


def reduce_first(pieces, others=None):
    cut = pieces[0].shape[0] // 2
    low, high = [p[:cut] for p in pieces], [p[cut:] for p in pieces]
    low_sent = jnp.concatenate([low[1], low[3]], axis=0)
    high_sent = jnp.concatenate([high[2], high[3]], axis=0)
    if others is not None:
        low_sent, high_sent = order([low_sent, high_sent], others)
    return low, high, swap(low_sent, "dp", 1), swap(high_sent, "dp", 2)


def reduce_step(state, between=None):
    low, high, low_got, high_got = state
    cut = low[0].shape[0]
    low_sum = (low[2].astype(f32) + low_got[cut:].astype(f32)).astype(bf16)
    high_sum = (high[1].astype(f32) + high_got[cut:].astype(f32)).astype(bf16)
    if between is not None:
        low_sum, high_sum = order([low_sum, high_sum], between)
    return swap(low_sum, "dp", 2), swap(high_sum, "dp", 1)


def reduce_end(state, low_next, high_next):
    low, high, low_got, high_got = state
    cut = low[0].shape[0]
    return jnp.concatenate(
        [
            total([low[0], low_got[:cut], low_next]).astype(bf16),
            total([high[0], high_got[:cut], high_next]).astype(bf16),
        ],
        axis=0,
    )


def reduce_second(state, between=None):
    return reduce_end(state, *reduce_step(state, between))


def gather_z(own_half):
    return jnp.concatenate(gather_rel(own_half, "expert")[1:], axis=0)


def along_z(others, own):
    tok = own.shape[0]
    count = others.shape[0] // tok
    pieces = [own] + [others[s * tok : (s + 1) * tok] for s in range(count)]
    return total(exchange_rel(pieces, "expert"))


def rows_join(own, other, core):
    rows = own.shape[0]
    result = jnp.zeros((2 * rows,) + own.shape[1:], own.dtype)
    result = lax.dynamic_update_slice_in_dim(result, own, core * rows, 0)
    return lax.dynamic_update_slice_in_dim(result, other, (1 - core) * rows, 0)


def feed_kernel(sh_width, width, padded, sub, at, n_own, n_oth, g_own, g_oth, gate_hbm, up_hbm, down_hbm,
                shared_hbm, *refs):
    hid_out, back_out, rows_own, rows_oth, out_own, out_oth, pre_w, down_w, sems = refs[-9:]
    half = n_own.shape[1]

    @pl.when(pl.program_id(0) == 0)
    def _():
        pick, core = at[0], at[1]
        copies = []
        for k in range(2):
            here = pl.multiple_of((core if k == 0 else 1 - core) * half, LANES)
            cols, to = pl.ds(here, half), pl.ds(k * half, half)
            moves = [
                (gate_hbm.at[pick, :, cols], pre_w.at[pl.ds(LANES, width), to]),
                (up_hbm.at[pick, :, cols], pre_w.at[pl.ds(padded + LANES, width), to]),
                (down_hbm.at[pick, :, cols], down_w.at[pl.ds(LANES, width), to]),
                (shared_hbm.at[pl.ds(0, LANES), cols], pre_w.at[pl.ds(0, LANES), to]),
                (shared_hbm.at[pl.ds(LANES, LANES), cols], pre_w.at[pl.ds(padded, LANES), to]),
                (shared_hbm.at[pl.ds(2 * LANES, LANES), cols], down_w.at[pl.ds(0, LANES), to]),
            ]
            for m, (source, target) in enumerate(moves):
                copies.append(pltpu.make_async_copy(source, target, sems.at[6 * k + m]))
        for copy in copies:
            copy.start()
        room = padded - LANES - width
        if room:
            zeros = jnp.zeros((room, 2 * half), bf16)
            pre_w[pl.ds(LANES + width, room), :] = zeros
            pre_w[pl.ds(padded + LANES + width, room), :] = zeros
            down_w[pl.ds(LANES + width, room), :] = zeros
        for copy in copies:
            copy.wait()

    lane = lax.broadcasted_iota(jnp.int32, (sub, LANES), 1)
    is_router = (lane >= sh_width) & (lane < sh_width + EXPERTS)
    is_own = lane == at[2]

    def activate(pre, up, back):
        sigmoid = 1.0 / (1.0 + jnp.exp(-pre))
        silu = pre * sigmoid
        slope = sigmoid + silu * (1.0 - sigmoid)
        return silu * up, back * up * slope, back * silu

    for start in range(0, n_own.shape[0], sub):
        rows = slice(start, start + sub)
        pre = mm_nt(n_own[rows], pre_w[:, :half]) + mm_nt(n_oth[rows], pre_w[:, half:])
        back = mm_nt(g_own[rows, :half], down_w[:, :half])
        back = back + mm_nt(g_oth[rows, :half], down_w[:, half:])
        gate_pre, up_pre = pre[:, :padded], pre[:, padded:]
        logits = jnp.where(is_router, up_pre[:, :LANES], masked_score)
        exps = jnp.exp(logits - jnp.max(logits, axis=1, keepdims=True))
        probs = exps / jnp.sum(exps, axis=1, keepdims=True)
        prob_own = jnp.sum(jnp.where(is_own, probs, 0.0), axis=1, keepdims=True)
        mask = g_own[rows, half:].astype(f32)
        routed = jnp.sum(jnp.where(is_own, mask, 0.0), axis=1, keepdims=True)
        gate = routed * prob_own
        hid_s, gg_s, gu_s = activate(gate_pre[:, :LANES], up_pre[:, :LANES], back[:, :LANES])
        hid, gg, gu = activate(gate_pre[:, LANES:], up_pre[:, LANES:], back[:, LANES:])
        prob_grad = routed * jnp.sum(hid * back[:, LANES:], axis=1, keepdims=True)
        logit_grad = probs * (jnp.where(is_own, prob_grad, 0.0) - prob_own * prob_grad)
        hid_out[rows, :LANES] = hid_s.astype(bf16)
        hid_out[rows, LANES:] = (hid * gate).astype(bf16)
        back_out[rows, :LANES] = gg_s.astype(bf16)
        back_out[rows, LANES:padded] = (gg * gate).astype(bf16)
        back_out[rows, padded : padded + LANES] = jnp.where(is_router, logit_grad, gu_s).astype(bf16)
        back_out[rows, padded + LANES :] = (gu * gate).astype(bf16)
        rows_oth[rows] = mm(back_out[rows], pre_w[:, half:]).astype(bf16)
        rows_own[rows] = mm(back_out[rows], pre_w[:, :half]).astype(bf16)
        out_oth[rows] = mm(hid_out[rows], down_w[:, half:]).astype(bf16)
        out_own[rows] = mm(hid_out[rows], down_w[:, :half]).astype(bf16)


def feed_call(at, sh_width, width, padded, rows_own, rows_other, grad_own, grad_other, weights, place, kept, others):
    tokens, half = rows_own.shape
    tile, sub = 256, 256
    by_rows = lambda m, at: (m, 0)
    first, every = place[0] // tile, place[1]
    placed_rows = lambda m, at: (m + first, 0)
    acts = [rows_own, rows_other, grad_own, grad_other]
    widths = [padded, 2 * padded, half, half, half, half]
    return pl.pallas_call(
        functools.partial(feed_kernel, sh_width, width, padded, sub),
        grid_spec=pltpu.PrefetchScalarGridSpec(
            num_scalar_prefetch=1,
            grid=(tokens // tile,),
            in_specs=[pl.BlockSpec((tile, a.shape[1]), by_rows) for a in acts]
            + [pl.BlockSpec(memory_space=pl.ANY) for w in weights + kept + others],
            out_specs=[
                pl.BlockSpec((tile, w), placed_rows if k < 2 else by_rows)
                for k, w in enumerate(widths)
            ],
            scratch_shapes=[
                pltpu.VMEM((2 * padded, 2 * half), bf16),
                pltpu.VMEM((padded, 2 * half), bf16),
                pltpu.SemaphoreType.DMA((12,)),
            ],
        ),
        out_shape=[
            jax.ShapeDtypeStruct((every if k < 2 else tokens, w), bf16)
            for k, w in enumerate(widths)
        ],
        input_output_aliases={9 + k: k for k in range(len(kept))},
        compiler_params=pltpu.CompilerParams(
            dimension_semantics=("arbitrary",), vmem_limit_bytes=58 * 1024 * 1024
        ),
        cost_estimate=pl.CostEstimate(
            flops=24 * tokens * half * padded,
            bytes_accessed=2 * tokens * (8 * half + 3 * padded) + 12 * half * padded,
            transcendentals=tokens * padded,
        ),
    )(at, *acts, *weights, *kept, *others)


def swap_quarters(values):
    lane = lax.broadcasted_iota(jnp.int32, values.shape, 1)
    return jnp.where(lane % 64 < 32, pltpu.roll(values, 96, 1), pltpu.roll(values, 32, 1))


def assemble(at, sources, x, wq, wl, up, wo, sems):
    x_rel, x_got, x_there, wl_there = sources[0], sources[1:4], sources[4:7], sources[7]
    pieces = [[sources[8]], [sources[9]], [sources[10]], list(sources[11:])]
    core, index = at[0], at[1]
    block = sources[8].shape[1]
    half, own, wl_rows = D // 2, x_rel.shape[0], wl_there.shape[0]
    up_rows = R // 4
    copies = []

    def copy(source, target):
        copies.append(pltpu.make_async_copy(source, target, sems.at[len(copies)]))

    def columns(which):
        return pl.ds(pl.multiple_of(which * half, LANES), half)

    def rows(first, unit, count):
        return pl.ds(pl.multiple_of(first * unit, 16), count)

    copy(x_rel, x.at[pl.ds(0, own)])
    for k in range(3):
        to = pl.ds((k + 1) * own, own)
        copy(x_got[k].at[:, pl.ds(0, half)], x.at[to, columns(core)])
        copy(x_there[k].at[:, pl.ds(0, half)], x.at[to, columns(1 - core)])
    copy(wl_there, wl.at[rows(1 - core, wl_rows, wl_rows)])
    fields = [wq.shape[0], wl_rows, up_rows, 0 if wo is None else wo.shape[0]]
    for s, parts in enumerate(pieces):
        base = 0
        for part in parts:
            start = 0
            for f, size in enumerate(fields):
                first, last = max(start, base), min(start + size, base + part.shape[0])
                if first < last:
                    source = part.at[pl.ds(first - base, last - first)]
                    off, count = first - start, last - first
                    to = pl.ds(s * block, block)
                    if f == 0:
                        copy(source, wq.at[pl.ds(off, count), to])
                    elif f == 1:
                        here = pl.multiple_of(core * wl_rows + off, 16)
                        copy(source, wl.at[pl.ds(here, count), to])
                    elif f == 2:
                        here = pl.multiple_of((index ^ s) * up_rows + off, 16)
                        copy(source, up.at[pl.ds(here, count)])
                    else:
                        copy(source, wo.at[pl.ds(off, count), to])
                start += size
            base += part.shape[0]
    for one in copies:
        one.start()
    for one in copies:
        one.wait()


def attend_kernel(at, *refs):
    sources, refs = refs[:13], refs[13:]
    (gain, cos, sin, mask, latent_gain, part_own, part_oth, normed_out, keys_out, queries_out, nope_out,
     probs_out, mixed_out, heads_out, unit_out, inverse_out, x, wq, wl, up, wo, sems) = refs
    assemble(at, sources, x, wq, wl, up, wo, sems)
    rows = x[...].astype(f32)
    normed = (rows * rms_stats(rows) * gain[...]).astype(bf16)
    normed_out[...] = normed
    query = mm_nt(normed, wq[...])
    latent_all = mm_nt(normed, wl[:R])
    inverse = rms_stats(latent_all)
    unit = latent_all * inverse
    unit_out[...] = unit
    inverse_out[...] = jnp.broadcast_to(inverse, inverse_out.shape)
    latent = (unit * latent_gain[...]).astype(bf16)
    key_rope = mm_nt(normed, jnp.concatenate([wl[R:], wl[R:]], axis=0))
    keys_out[:, :R] = latent
    keys_out[:, R:] = (key_rope * cos[...] + swap_quarters(key_rope) * sin[...]).astype(bf16)
    ropes = query[:, 2 * DN :]
    ropes = (ropes * cos[...] + swap_quarters(ropes) * sin[...]).astype(bf16)
    lane = lax.broadcasted_iota(jnp.int32, ropes.shape, 1)
    keys = keys_out[...]
    allowed = mask[...] > 0
    for h in range(2):
        nope = query[:, h * DN : (h + 1) * DN].astype(bf16)
        nope_out[:, h * DN : (h + 1) * DN] = nope
        queries_out[h, :, :R] = mm_nt(nope, up[:, h * (DN + DV) : h * (DN + DV) + DN]).astype(bf16)
        queries_out[h, :, R:] = jnp.where(lane // 64 == h, ropes, jnp.zeros_like(ropes))
        scores = mm_nt(queries_out[h], keys) * (DN + DR) ** (-0.5)
        scores = jnp.where(allowed, scores, masked_score)
        exps = jnp.exp(scores - jnp.max(scores, axis=1, keepdims=True))
        probs = exps / jnp.sum(exps, axis=1, keepdims=True)
        probs_out[h] = probs
        mixed = mm(probs.astype(bf16), latent).astype(bf16)
        mixed_out[h] = mixed
        heads_out[:, h * DV : (h + 1) * DV] = mm(
            mixed, up[:, h * (DN + DV) + DN : (h + 1) * (DN + DV)]
        ).astype(bf16)
    half = part_own.shape[1]
    part = mm(heads_out[...], wo[...]).astype(bf16)
    first = at[0] == 0
    part_own[...] = jnp.where(first, part[:, :half], part[:, half:])
    part_oth[...] = jnp.where(first, part[:, half:], part[:, :half])


def attend_back_kernel(at, *refs):
    sources, refs = refs[:13], refs[13:]
    (res, normed, cos, sin, latent_gain, keys, queries, nope, probs, mixed, heads, unit, inverse,
     back_own, back_oth, grad_wo, grad_wq, grad_wl, grad_wl_oth, grad_up, grad_gain, grad_latent_gain,
     gl_ref, gq_ref, gk_ref, x, wq, wl, up, wo, sems) = refs
    assemble(at, sources, x, wq, wl, up, wo, sems)
    res_rows = res[...]
    grad_wo[...] = mm_tn(heads[...], res_rows).astype(bf16)
    grad_heads = mm_nt(res_rows, wo[...]).astype(bf16)
    latent = keys[:, :R]
    lane = lax.broadcasted_iota(jnp.int32, cos.shape, 1)
    grad_ropes = jnp.zeros(cos.shape, f32)
    uw = DN + DV
    for h in range(2):
        grad_head = grad_heads[:, h * DV : (h + 1) * DV]
        up_key = up[:, h * uw : h * uw + DN]
        grad_mixed = mm_nt(grad_head, up[:, h * uw + DN : (h + 1) * uw]).astype(bf16)
        prob = probs[h]
        grad_att = mm_nt(grad_mixed, latent)
        delta = jnp.sum(prob * grad_att, axis=1, keepdims=True)
        score_grad = (prob * (grad_att - delta) * (DN + DR) ** (-0.5)).astype(bf16)
        grad_query = mm(score_grad, keys[...])
        grad_keys = mm_tn(score_grad, queries[h])
        grad_latent = grad_keys[:, :R] + mm_tn(prob.astype(bf16), grad_mixed)
        if h == 0:
            gk_ref[:, :R] = grad_latent
            gk_ref[:, R:] = grad_keys[:, R:]
        else:
            gk_ref[:, :R] += grad_latent
            gk_ref[:, R:] += grad_keys[:, R:]
        grad_ropes = grad_ropes + jnp.where(lane // 64 == h, grad_query[:, R:], 0.0)
        grad_ql = grad_query[:, :R].astype(bf16)
        gq_ref[:, h * DN : (h + 1) * DN] = mm(grad_ql, up_key).astype(bf16)
        grad_up[h * uw : h * uw + DN] = mm_tn(nope[:, h * DN : (h + 1) * DN], grad_ql).astype(bf16)
        grad_up[h * uw + DN : (h + 1) * uw] = mm_tn(grad_head, mixed[h]).astype(bf16)
    gq_ref[:, 2 * DN :] = (grad_ropes * cos[...] - swap_quarters(grad_ropes) * sin[...]).astype(bf16)
    grad_latent = gk_ref[:, :R]
    grad_latent_gain[...] = jnp.sum(grad_latent * unit[...], axis=0, keepdims=True)
    gl_ref[:, :R] = rms_back(grad_latent * latent_gain[...], unit[...], inverse[:, :1]).astype(bf16)
    key_ropes = gk_ref[:, R:]
    key_ropes = key_ropes + pltpu.roll(key_ropes, 64, 1)
    key_ropes = key_ropes * cos[...] - swap_quarters(key_ropes) * sin[...]
    gl_ref[:, R:] = key_ropes.astype(bf16)
    back = mm(gq_ref[...], wq[...]) + mm(gl_ref[:, :R], wl[:R]) + mm(gl_ref[:, R : R + DR], wl[R:])
    tree_rows = x[...].astype(f32)
    unit_rows = tree_rows * rms_stats(tree_rows)
    grad_gain[...] = jnp.sum(back * unit_rows, axis=0, keepdims=True)
    half = back_own.shape[1]
    back = back.astype(bf16)
    first = at[0] == 0
    back_own[...] = jnp.where(first, back[:, :half], back[:, half:])
    back_oth[...] = jnp.where(first, back[:, half:], back[:, :half])
    rows = normed[...]
    grad_wq[...] = mm_tn(gq_ref[...], rows).astype(bf16)
    cut = grad_wl.shape[0]
    low = mm_tn(gl_ref[:, : 3 * LANES], rows).astype(bf16)
    high = mm_tn(gl_ref[:, 2 * LANES :], rows).astype(bf16)
    low, high = low[:cut], high[cut - 2 * LANES : 2 * cut - 2 * LANES]
    grad_wl[...] = jnp.where(first, low, high)
    grad_wl_oth[...] = jnp.where(first, high, low)


def whole_call(kernel, sources, operands, outs, scratch, at, tree_len, wq_rows, wo_rows):
    scratch = scratch + [
        pltpu.VMEM((tree_len, D), bf16),
        pltpu.VMEM((wq_rows, D), bf16),
        pltpu.VMEM((R + DR, D), bf16),
        pltpu.VMEM((R, R), bf16),
        pltpu.VMEM((wo_rows, D), bf16),
        pltpu.SemaphoreType.DMA((32,)),
    ]
    return pl.pallas_call(
        kernel,
        in_specs=[pl.BlockSpec(memory_space=pltpu.SMEM)]
        + [pl.BlockSpec(memory_space=pl.ANY)] * len(sources)
        + [pl.BlockSpec(memory_space=pltpu.VMEM)] * len(operands),
        out_specs=[pl.BlockSpec(memory_space=pltpu.VMEM)] * len(outs),
        out_shape=[jax.ShapeDtypeStruct(shape, kind) for shape, kind in outs],
        scratch_shapes=scratch,
        compiler_params=pltpu.CompilerParams(vmem_limit_bytes=58 * 1024 * 1024),
        cost_estimate=pl.CostEstimate(flops=0, bytes_accessed=0, transcendentals=0),
    )(at, *sources, *operands)


def weight_kernel(segments, at, lefts, owns, others, out):
    c = pl.program_id(0)
    mine = (c // (pl.num_programs(0) // 2)) == at[0]

    def run(rights):
        to = 0
        for start, rows in segments:
            result = jnp.zeros((rows, out.shape[1]), f32)
            first = 0
            for right in rights:
                deep = right.shape[0]
                result = result + mm_tn(lefts[first : first + deep, start : start + rows], right[...])
                first += deep
            out[to : to + rows] = result.astype(bf16)
            to += rows

    @pl.when(mine)
    def _():
        run(owns)

    @pl.when(jnp.logical_not(mine))
    def _():
        run(others)


def weight_call(core, left, owns, others, segments, count):
    block = D // count
    rows = sum(size for first, size in segments)
    per_half = count // 2

    def body(at, *refs):
        parts = len(owns)
        weight_kernel(segments, at, refs[0], refs[1 : 1 + parts], refs[1 + parts : -1], refs[-1])

    columns = lambda c, at: (0, c % per_half)
    return pl.pallas_call(
        body,
        grid_spec=pltpu.PrefetchScalarGridSpec(
            num_scalar_prefetch=1,
            grid=(count,),
            in_specs=[pl.BlockSpec(left.shape, lambda c, at: (0, 0), pipeline_mode=pl.Buffered(1))]
            + [pl.BlockSpec((r.shape[0], block), columns) for r in owns + others],
            out_specs=pl.BlockSpec((rows, block), lambda c, at: (c, 0)),
        ),
        out_shape=jax.ShapeDtypeStruct((count * rows, block), bf16),
        compiler_params=pltpu.CompilerParams(
            dimension_semantics=("arbitrary",), vmem_limit_bytes=58 * 1024 * 1024
        ),
        cost_estimate=pl.CostEstimate(flops=0, bytes_accessed=0, transcendentals=0),
    )(jnp.reshape(core, (1,)).astype(jnp.int32), left, *owns, *others)


def per_device(
    layer_in,
    norm_gain,
    query_proj,
    latent_proj,
    latent_gain,
    latent_up,
    output_proj,
    ffn_gain,
    router,
    shared_gate,
    shared_up,
    shared_down,
    expert_gate,
    expert_up,
    expert_down,
    routes,
    leaf_parent,
    grad_out,
):
    tok = layer_in.shape[0]
    n_dp, n_ex = lax.axis_size("dp"), lax.axis_size("expert")
    i, j, core = lax.axis_index("dp"), lax.axis_index("expert"), lax.axis_index("tensor")
    tree_len = tok * n_ex
    seg_len = tree_len // 16
    trunk_len = 4 * seg_len
    block = D // n_dp
    sub = block // n_ex
    heads_local = output_proj.shape[0] // DV
    groups = min(n_ex, heads_local)
    hp = heads_local // groups
    qg = n_ex // groups
    group = j // qg
    n_q = n_ex // qg
    rows_q = tok * n_q
    qw = DN + DR
    uw = DN + DV
    score_scale = (DN + DR) ** (-0.5)

    x_rel = permute_blocks(layer_in, i, n_dp)
    gain_one = permute_blocks(norm_gain.astype(f32), i, n_dp)
    gain_two = permute_blocks(ffn_gain.astype(f32), i, n_dp)
    gain_latent = latent_gain.astype(f32)
    half = D // 2
    up_rows = R // n_dp
    by_kernel = qg == 1 and hp == 2 and tree_len <= 512 and n_ex == 4
    sh_width = shared_gate.shape[1] // (n_dp * n_ex)
    lanes = jnp.arange(LANES, dtype=jnp.int32) - sh_width
    route_lanes = jnp.any(routes[:, :, None] == lanes[None, None, :], axis=1).astype(bf16)

    def with_grad(which):
        return jnp.concatenate(
            [pick_half(x_rel, which, 1), pick_half(grad_out, which, 1), route_lanes], axis=1
        )

    xg_own, xg_other = with_grad(core), with_grad(1 - core)
    xg_got = gather_rel(xg_own, "expert")[1:]
    xg_there = [swap(p, "tensor", 1) for p in xg_got]
    grad_wide = half + LANES

    def grad_rows_of(got, own):
        return place_rows(
            [(p, 0, tok, k * tok, 0, (half, grad_wide)) for k, p in enumerate(got + [own])], tree_len
        )

    g_rows = grad_rows_of(xg_got, xg_own)
    wq_rows, wl_rows = hp * qw, (R + DR) // 2
    if by_kernel:
        at_pack = jnp.stack([group, core]).astype(jnp.int32)
        packed = pack_call(at_pack, query_proj, latent_proj.T, latent_up, output_proj, block)
        first = gather_parts(packed, xg_got)
        wl_parts = []
        for s, piece in enumerate(first):
            base = 0
            for part in piece:
                low = max(wq_rows, base)
                high = min(wq_rows + wl_rows, base + part.shape[0])
                if low < high:
                    wl_parts.append((part, low - base, high - low, low - wq_rows, s * block))
                base += part.shape[0]
        wl_there = swap(place_rows(wl_parts, wl_rows), "tensor", 1)
        gathered = [x_rel] + xg_got + xg_there + [wl_there] + [p for piece in first for p in piece]
        ready = first[3]
    else:
        wq_own = lax.dynamic_slice_in_dim(query_proj, group * hp * qw, hp * qw, 1).T
        wl_own = pick_half(latent_proj.T, core, 0)
        up_own = lax.dynamic_slice_in_dim(latent_up, group * hp * uw, hp * uw, 1)
        wo_own = lax.dynamic_slice_in_dim(output_proj, group * hp * DV, hp * DV, 0)
        x_got = jnp.concatenate([p[:, :half] for p in xg_got], axis=0)
        x_there = jnp.concatenate([p[:, :half] for p in xg_there], axis=0)
        wq = jnp.concatenate(gather_dp(wq_own), axis=1)
        wl_got = jnp.concatenate(gather_dp(wl_own), axis=1)
        wl = rows_join(wl_got, swap(wl_got, "tensor", 1), core)
        up = jnp.concatenate(canonical(gather_rel(up_own, "dp"), i), axis=0)
        wo = jnp.concatenate(gather_rel(wo_own, "dp"), axis=1)
        x_tree = jnp.concatenate([x_rel, halves(x_got, x_there, core, 1)], axis=0)
        ready = [wq, wo]

    local_experts = expert_gate.shape[0]
    parts = n_dp // local_experts
    width = expert_gate.shape[2] // parts
    chosen, part_at = i // parts, (i % parts) * width
    expert_id = j * local_experts + chosen
    sh_sent = []
    for c in range(n_dp):
        at_unit = (j * n_dp + c) * sh_width
        sh_sent += [
            lax.dynamic_slice_in_dim(shared_gate, at_unit, sh_width, 1).T,
            lax.dynamic_slice_in_dim(shared_up, at_unit, sh_width, 1).T,
            lax.dynamic_slice_in_dim(shared_down, at_unit, sh_width, 0),
        ]
    sh_sent = order([jnp.concatenate(sh_sent, axis=0)], ready)[0]
    sh_got = lax.all_to_all(sh_sent, "dp", 0, 0, tiled=True)
    sh_rows = jnp.concatenate(
        [sh_got[c * 3 * sh_width : (c + 1) * 3 * sh_width] for c in range(n_dp)], axis=1
    )
    hidden_width = -(-(LANES + width) // LANES) * LANES

    room = LANES - sh_width
    shared_w = jnp.concatenate(
        [
            jnp.pad(sh_rows[:sh_width], ((0, room), (0, 0))),
            sh_rows[sh_width : 2 * sh_width],
            router.T,
            jnp.zeros((room - EXPERTS, D), bf16),
            jnp.pad(sh_rows[2 * sh_width :], ((0, room), (0, 0))),
        ],
        axis=0,
    )
    feed_weights = [jnp.swapaxes(expert_gate, 1, 2), jnp.swapaxes(expert_up, 1, 2), expert_down]
    pick = chosen
    if parts > 1:
        feed_weights = [lax.dynamic_slice(w, (chosen, part_at, 0), (1, width, D)) for w in feed_weights]
        pick = chosen * 0
    feed_weights = feed_weights + [shared_w]

    slots = jnp.arange(tree_len, dtype=jnp.int32)
    token_index = (j ^ (slots // tok)) * tok + slots % tok

    def queries_of(values):
        if qg == 1:
            return values
        split = values.reshape((n_q, qg, tok) + values.shape[1:])[:, 0]
        return split.reshape((rows_q,) + values.shape[1:])

    position, segment, parent, grand = tree_layout(leaf_parent, token_index, trunk_len, seg_len)
    freqs = 10000.0 ** (-2.0 * jnp.arange(DR // 2, dtype=f32) / DR)
    angles = position.astype(f32)[:, None] * freqs[None, :]
    cosine, sine = jnp.cos(angles), jnp.sin(angles)
    q_cos, q_sin = queries_of(cosine), queries_of(sine)
    allowed = visible(
        queries_of(segment),
        queries_of(parent),
        queries_of(grand),
        queries_of(token_index),
        segment,
        token_index,
    )

    own_rows = x_rel.astype(f32)
    inverse_one = rms_stats(own_rows)
    unit_one = own_rows * inverse_one
    at_all = jnp.stack([core, i]).astype(jnp.int32)
    if by_kernel:
        cos_lanes = jnp.concatenate([cosine] * 4, axis=1)
        sin_lanes = jnp.concatenate([-sine, sine] * 2, axis=1)
        rows, wide = tree_len, (tree_len, LANES)
        (
            part_own, part_other, normed, keys, queries, nope, probs, mixed, heads_out, unit_latent,
            inverse_latent,
        ) = whole_call(
            attend_kernel,
            gathered,
            [
                gain_one[None], cos_lanes, sin_lanes, allowed.astype(bf16),
                gain_latent[None],
            ],
            [
                ((rows, half), bf16), ((rows, half), bf16),
                ((rows, D), bf16), ((rows, R + LANES), bf16), ((2, rows, R + LANES), bf16),
                ((rows, 2 * DN), bf16), ((2, rows, rows), f32), ((2, rows, R), bf16),
                ((rows, 2 * DV), bf16), ((rows, R), f32), (wide, f32),
            ],
            [],
            at_all, tree_len, wq_rows, hp * DV,
        )
        part_other = order([part_other], [sh_got])[0]
    else:
        tree_unit = x_tree.astype(f32)
        tree_unit = tree_unit * rms_stats(tree_unit)
        normed = (tree_unit * gain_one).astype(bf16)
        normed_q = queries_of(normed)
        query_all = mm_nt(normed_q, wq)
        latent_all = mm_nt(normed, wl)
        inverse_latent = rms_stats(latent_all[:, :R])
        unit_latent = latent_all[:, :R] * inverse_latent
        latent = (unit_latent * gain_latent).astype(bf16)
        key_rope = rotate(latent_all[:, R:], cosine, sine).astype(bf16)
        keys = jnp.concatenate([latent, key_rope], axis=1)
        up_key = [up[:, h * uw : h * uw + DN] for h in range(hp)]
        up_value = [up[:, h * uw + DN : (h + 1) * uw] for h in range(hp)]
        query_nope = [query_all[:, h * qw : h * qw + DN].astype(bf16) for h in range(hp)]
        queries = jnp.concatenate(
            [
                jnp.concatenate(
                    [
                        mm_nt(query_nope[h], up_key[h]).astype(bf16),
                        rotate(query_all[:, h * qw + DN : (h + 1) * qw], q_cos, q_sin).astype(bf16),
                    ],
                    axis=1,
                )
                for h in range(hp)
            ],
            axis=0,
        )
        raw_scores = mm_nt(queries, keys).reshape(hp, rows_q, tree_len)
        scores = jnp.where(allowed[None], raw_scores * score_scale, masked_score)
        exp_scores = jnp.exp(scores - jnp.max(scores, axis=-1, keepdims=True))
        probs = exp_scores / jnp.sum(exp_scores, axis=-1, keepdims=True)
        probs = probs.reshape(hp * rows_q, tree_len)
        probs_low = probs.astype(bf16)
        mixed = mm(probs_low, latent).astype(bf16)
        mixed_head = [mixed[h * rows_q : (h + 1) * rows_q] for h in range(hp)]
        heads_out = jnp.concatenate(
            [mm(mixed_head[h], up_value[h]).astype(bf16) for h in range(hp)], axis=1
        )
        part_own, part_other = mm(heads_out, pick_half(wo, core, 1)), mm(
            heads_out, pick_half(wo, 1 - core, 1)
        )

    g_parts = gather_parts(g_rows)

    def tree_scatter(partial_own, partial_other, count, stride, before=None):
        there = swap(partial_other.astype(bf16), "tensor", 1)
        joined = (partial_own.astype(f32) + there.astype(f32)).astype(bf16)
        own = total(
            exchange_rel(
                [joined[s * tok : (s + 1) * tok] for s in range(count)], "expert", stride
            )
        )
        if before is not None:
            own = order([own], before)[0]
        return halves(own, swap(own, "tensor", 1), core, 1)

    attention = tree_scatter(part_own, part_other, n_q, qg, g_parts[1] + g_parts[2])
    residual = own_rows + attention
    inverse_two = rms_stats(residual)
    unit_two = residual * inverse_two
    normed_two = permute_blocks((unit_two * gain_two).astype(bf16), i, n_dp)

    n_half = pick_half(normed_two, core, 1)
    n_other = pick_half(normed_two, 1 - core, 1)
    n_others = join_rows(gather_rel(n_half, "expert")[1:])
    own_parts = gather_parts(n_half)
    n_others = order([n_others], g_parts[3] + own_parts[1] + own_parts[2])[0]
    n_there = swap(n_others, "tensor", 1)
    g_rest = join_rows(g_parts[1] + g_parts[2] + g_parts[3])
    grad_own = [g_rows, g_rest]
    grad_other = [grad_rows_of(xg_there, xg_other), swap(g_rest, "tensor", 1)]
    at = jnp.stack([pick, core, sh_width + expert_id]).astype(jnp.int32)
    tree_rows = n_others.shape[0] + tok
    tokens = tree_rows * n_dp

    def feed(k, own, other, kept, others):
        return feed_call(
            at, sh_width, width, hidden_width, own, other, grad_own[k], grad_other[k],
            feed_weights, (k * tree_rows, tokens), kept, others,
        )

    rows_own = [join_rows([n_others, n_half])]
    rows_other = [join_rows([n_there, n_other])]
    made = feed(0, rows_own[0], rows_other[0], [], [])
    other_parts = gather_parts(n_others, [made[0]])
    near = join_rows(
        other_parts[1] + own_parts[1] + other_parts[2] + own_parts[2], [made[0]]
    )
    far = join_rows(other_parts[3] + own_parts[3])
    rows_own.append(join_rows([near, far]))
    rows_other.append(join_rows([swap(near, "tensor", 1), swap(far, "tensor", 1)]))
    grad_parts, out_parts = [made[2:4]], [made[4:6]]
    theirs = [swap(made[3], "tensor", 1)]
    out_there = [swap(made[5], "tensor", 1)]
    made = feed(1, rows_own[1], rows_other[1], list(made[:2]), theirs + out_there)
    grad_parts.append(made[2:4])
    out_parts.append(made[4:6])
    hidden_scaled, back_pre = made[:2]

    def join(mine, theirs):
        return (mine.astype(f32) + swap(theirs, "tensor", 1).astype(f32)).astype(bf16)

    routed_at, up_at = (LANES, width), (hidden_width + LANES, width)
    sent_width = -(-sh_width // 16) * 16
    sent_router = -(-(sh_width + EXPERTS) // 16) * 16

    theirs.append(swap(grad_parts[1][1], "tensor", 1))
    many = tree_rows - tok

    def joined(mine, there, low, high):
        return (mine[low:high].astype(f32) + there[low:high].astype(f32)).astype(bf16)

    def cut_of(parts, there, low, high):
        return [joined(parts[0], there[0], low, high)] + [
            joined(parts[1], there[1], s * tree_rows + low, s * tree_rows + high)
            for s in range(n_dp - 1)
        ]

    grad_mine = [p[0] for p in grad_parts]
    hidden_late = order([hidden_scaled], [theirs[1]])[0]
    down_sent = weight_call(
        core, hidden_late, grad_own, grad_other, [routed_at, (0, sent_width)], n_dp
    )
    others_state = reduce_first(cut_of(grad_mine, theirs, 0, many))
    others_first = list(others_state[2:])
    back_late = order([back_pre], others_first)[0]
    gate_sent = weight_call(
        core, back_late, rows_own, rows_other,
        [routed_at, (0, sent_width), (hidden_width, sent_router)], n_dp,
    )
    own_state = reduce_first(cut_of(grad_mine, theirs, many, tree_rows), others_first)
    gn2_others = reduce_second(others_state, [down_sent])
    gn2_own = order([reduce_second(own_state)], [gate_sent])[0]

    out_there.append(swap(order([out_parts[1][1]], [theirs[1]])[0], "tensor", 1))
    out_state = reduce_first(
        cut_of([p[0] for p in out_parts], out_there, 0, tree_rows), [gn2_own]
    )
    out_first = list(out_state[2:])
    z_sent = gn2_others
    z_got = exchange_rel(
        [gn2_own] + [z_sent[s * tok : (s + 1) * tok] for s in range(n_ex - 1)], "expert"
    )
    back_last = order([back_late], [z_got[1]])[0]
    up_sent = weight_call(core, back_last, rows_own, rows_other, [up_at], n_dp)
    gn2_half = order([total(z_got)], [up_sent])[0]
    gn2 = permute_blocks(halves(gn2_half, swap(gn2_half, "tensor", 1), core, 1), i, n_dp)

    grad_ffn_gain = jnp.sum(gn2 * unit_two, axis=0, keepdims=True)
    grad_residual = permute_blocks(grad_out, i, n_dp).astype(f32) + rms_back(
        gn2 * gain_two, unit_two, inverse_two
    )
    res_half = pick_half(grad_residual.astype(bf16), core, 1)

    out_last = list(reduce_step(out_state))
    out_mine = reduce_end(out_state, *out_last)
    out_got = exchange_rel(
        [out_mine[many:]] + [out_mine[s * tok : (s + 1) * tok] for s in range(n_ex - 1)], "expert"
    )

    def to_owners(sent, others):
        sent = order([sent], others)[0]
        return lax.all_to_all(sent, "dp", 0, 0, tiled=True).reshape(n_dp, -1, block)

    down_got = to_owners(down_sent, [gn2_own])
    gate_got = to_owners(gate_sent, [gn2_half])
    up_got = to_owners(up_sent, [gn2_half])
    router_at = width + sent_width + sh_width
    router_block = gate_sent.reshape(n_dp, -1, block)[:, router_at : router_at + EXPERTS]
    grad_router_rows = jnp.concatenate(
        [lax.dynamic_index_in_dim(router_block, i ^ s, 0, False) for s in range(n_dp)], axis=1
    )

    res_others = order([gather_z(res_half)], out_first)[0]
    res_others = halves(res_others, swap(res_others, "tensor", 1), core, 1)
    res_tree = jnp.concatenate([grad_residual.astype(bf16), res_others], axis=0)
    res_tree = order([res_tree], out_last)[0]
    if by_kernel:
        (
            back_mine, back_other, grad_wo, wq_grad, wl_grad, wl_sent, by_r, grad_norm_gain,
            grad_latent_gain,
        ) = (
            whole_call(
                attend_back_kernel,
                gathered,
                [
                    res_tree, normed, cos_lanes, sin_lanes, gain_latent[None], keys, queries, nope,
                    probs, mixed, heads_out, unit_latent, inverse_latent,
                ],
                [
                    ((rows, half), bf16), ((rows, half), bf16), ((2 * DV, D), bf16),
                    ((2 * qw, D), bf16), ((wl_rows, D), bf16), ((wl_rows, D), bf16),
                    ((2 * uw, R), bf16), ((1, D), f32),
                    ((1, R), f32),
                ],
                [
                    pltpu.VMEM((rows, R + LANES), bf16),
                    pltpu.VMEM((rows, 2 * qw), bf16),
                    pltpu.VMEM((rows, R + LANES), f32),
                ],
                at_all, tree_len, wq_rows, hp * DV,
            )
        )
    else:
        res_q = res_tree
        res_q = queries_of(res_q)
        grad_heads = mm_nt(res_q, wo).astype(bf16)
        grad_head = [grad_heads[:, h * DV : (h + 1) * DV] for h in range(hp)]

        grad_wo = mm_tn(heads_out, res_q)

        grad_mixed = jnp.concatenate(
            [mm_nt(grad_head[h], up_value[h]).astype(bf16) for h in range(hp)], axis=0
        )
        grad_att = mm_nt(grad_mixed, latent)
        delta = jnp.sum(probs * grad_att, axis=-1, keepdims=True)
        score_grad = (probs * (grad_att - delta) * score_scale).astype(bf16)
        grad_queries = mm(score_grad, keys)
        grad_keys = mm_tn(score_grad, queries)
        grad_latent_keys = grad_keys[:, :R] + mm_tn(probs_low, grad_mixed)
        grad_query_latent = grad_queries[:, :R].astype(bf16)
        grad_query_parts, grad_up_parts = [], []
        for h in range(hp):
            rows = slice(h * rows_q, (h + 1) * rows_q)
            grad_query_parts.append(mm(grad_query_latent[rows], up_key[h]))
            grad_query_parts.append(rotate_back(grad_queries[rows, R:], q_cos, q_sin))
            grad_up_parts.append(mm_tn(query_nope[h], grad_query_latent[rows]))
            grad_up_parts.append(mm_tn(grad_head[h], mixed_head[h]))
        grad_query_all = jnp.concatenate(grad_query_parts, axis=1).astype(bf16)
        grad_latent_gain = jnp.sum(grad_latent_keys * unit_latent, axis=0, keepdims=True)
        grad_latent_all = jnp.concatenate(
            [
                rms_back(grad_latent_keys * gain_latent, unit_latent, inverse_latent),
                rotate_back(grad_keys[:, R:], cosine, sine),
            ],
            axis=1,
        ).astype(bf16)

        grad_query_rows = grad_query_all
        if qg > 1:
            grad_query_rows = jnp.pad(
                grad_query_all.reshape(n_q, 1, tok, -1), ((0, 0), (0, qg - 1), (0, 0), (0, 0))
            ).reshape(tree_len, -1)
        def back_half(which):
            return mm(grad_query_rows, pick_half(wq, which, 1)) + mm(
                grad_latent_all, pick_half(wl, which, 1)
            )

        back_mine, back_other = back_half(core), back_half(1 - core)
        norm_mine = jnp.sum(back_mine * pick_half(tree_unit, core, 1), axis=0, keepdims=True)
        norm_other = jnp.sum(back_other * pick_half(tree_unit, 1 - core, 1), axis=0, keepdims=True)
        grad_norm_gain = halves(norm_mine, norm_other, core, 1)
        wq_grad, wl_grad = mm_tn(grad_query_all, normed_q), mm_tn(grad_latent_all, normed)
        by_r = jnp.concatenate(grad_up_parts, axis=0)


    up_sub = up_rows // n_ex
    gain_row = jnp.concatenate(
        [
            lax.dynamic_slice_in_dim(grad_latent_gain, (i ^ s) * up_rows, up_rows, 1)
            for s in range(n_dp)
        ],
        axis=1,
    ).reshape(n_dp * n_ex, up_sub)
    gain_row = jnp.pad(gain_row, ((0, 0), (0, sub - up_sub))).reshape(1, D)
    if not by_kernel:
        wl_grad = wl_grad.astype(bf16)
        wl_grad, wl_sent = pick_half(wl_grad, core, 0), pick_half(wl_grad, 1 - core, 0)
    wl_there = swap(wl_sent, "tensor", 1)
    wl_grad = wl_grad.astype(f32) + wl_there.astype(f32)
    small_rows = jnp.concatenate(
        [
            grad_norm_gain,
            0.5 * grad_ffn_gain,
            grad_router_rows.astype(f32),
            gain_row,
            jnp.zeros((13, D), f32),
        ],
        axis=0,
    )
    by_d = [grad_wo, wq_grad, wl_grad, small_rows]
    by_r = by_r.astype(bf16)
    d_rows, r_rows = sum(p.shape[0] for p in by_d), by_r.shape[0]
    by_r = [lax.dynamic_slice_in_dim(by_r, (i ^ s) * up_rows, up_rows, 1) for s in range(n_dp)]
    split_r = block // up_rows
    cut_r = r_rows // split_r
    by_r = jnp.concatenate(
        [
            jnp.concatenate([by_r[s][c * cut_r : (c + 1) * cut_r] for c in range(split_r)], 1)
            for s in range(n_dp)
        ],
        axis=1,
    )
    tail_state = reduce_first(stack_rows(by_d + [by_r], block))
    back_other = order([back_other], out_got[1:] + [down_got])[0]
    grad_normed = tree_scatter(back_mine, back_other, n_ex, 1, list(tail_state[2:]) + [gate_got])
    grad_in = permute_blocks(
        grad_residual + rms_back(grad_normed * gain_one, unit_one, inverse_one), i, n_dp
    )

    mine = reduce_second(tail_state)
    ffn_half = total(out_got)
    out_half = (pick_half(permute_blocks(residual, i, n_dp), core, 1) + ffn_half).astype(bf16)
    layer_out = halves(out_half, swap(out_half, "tensor", 1), core, 1)

    mine_r = jnp.concatenate(
        [mine[d_rows:, c * up_rows : (c + 1) * up_rows] for c in range(split_r)], axis=0
    )

    def z_piece(s):
        to = j ^ s
        rows_r = lax.dynamic_slice_in_dim(mine_r, to * up_sub, up_sub, 1)
        cut = r_rows * up_sub // sub
        return jnp.concatenate(
            [lax.dynamic_slice_in_dim(mine[:d_rows], to * sub, sub, 1)]
            + [
                jnp.concatenate(
                    [rows_r[c * cut : (c + 1) * cut] for c in range(sub // up_sub)], axis=1
                )
            ],
            axis=0,
        )

    got = exchange_rel([z_piece(s) for s in range(n_ex)], "expert")

    def over_groups(pieces):
        ordered = canonical(pieces, j)
        return jnp.concatenate(
            [total(ordered[g * qg : (g + 1) * qg]) for g in range(groups)], axis=0
        )

    ends = [hp * DV, hp * DV + wq_rows, hp * DV + wq_rows + wl_rows]
    grad_output_proj = over_groups([p[: ends[0]] for p in got])
    grad_query_rows = [p[ends[0] : ends[1]] for p in got]
    if by_kernel:
        grad_query_rows = [
            jnp.concatenate(
                [p[:DN], p[2 * DN : 2 * DN + DR], p[DN : 2 * DN], p[2 * DN + DR :]], axis=0
            )
            for p in grad_query_rows
        ]
    grad_query_proj = over_groups(grad_query_rows).T
    grad_latent_up = over_groups(
        [
            jnp.concatenate(
                [p[d_rows:, c * up_sub : (c + 1) * up_sub] for c in range(sub // up_sub)], axis=0
            )
            for p in got
        ]
    ).T
    rest = order([total([p[ends[1] : d_rows] for p in got])], [up_got])[0]
    rest_there = swap(rest, "tensor", 1)
    grad_latent_proj = rows_join(rest[:wl_rows], rest_there[:wl_rows], core).T
    small = rest[wl_rows:] + rest_there[wl_rows:]

    down_got, gate_got = order([down_got, gate_got], [grad_normed])
    shared_all = jnp.concatenate(
        [gate_got[:, width : width + 2 * sent_width], down_got[:, width:]], axis=1
    )
    shared_all = jnp.stack(
        canonical(
            exchange_rel(
                [lax.dynamic_slice_in_dim(shared_all, (j ^ s) * sub, sub, 2) for s in range(n_ex)],
                "expert",
            ),
            j,
        )
    )

    def shared_part(k):
        rows = shared_all[:, :, k * sent_width : k * sent_width + sh_width]
        return rows.reshape(-1, sub).astype(f32)

    def expert_part(got):
        return got[:, :width].reshape(local_experts, parts * width, block).astype(f32)

    grad_shared_gate, grad_shared_up = shared_part(0).T, shared_part(1).T
    grad_shared_down = shared_part(2)
    grad_expert_gate = jnp.swapaxes(expert_part(gate_got), 1, 2)
    grad_expert_up = jnp.swapaxes(expert_part(up_got), 1, 2)
    grad_expert_down = expert_part(down_got)

    return (
        layer_out,
        grad_in,
        small[0],
        grad_query_proj,
        grad_latent_proj,
        small[2 + EXPERTS, :up_sub],
        grad_latent_up,
        grad_output_proj,
        small[1],
        small[2 : 2 + EXPERTS].T,
        grad_shared_gate,
        grad_shared_up,
        grad_shared_down,
        grad_expert_gate,
        grad_expert_up,
        grad_expert_down,
    )


def solution(mesh):
    placed = (
        P(("dp", "expert"), None),
        P(),
        P("dp", "tensor"),
        P("dp", None),
        P(),
        P("dp", "tensor"),
        P("tensor", "dp"),
        P(),
        P(),
        P("dp", "tensor"),
        P("dp", "tensor"),
        P("tensor", "dp"),
        P("expert", None, "tensor"),
        P("expert", None, "tensor"),
        P("expert", "tensor", None),
        P(("dp", "expert"), None),
        P(),
        P(("dp", "expert"), None),
    )
    return jax.shard_map(
        per_device,
        mesh=mesh,
        in_specs=placed,
        out_specs=(
            P(("dp", "expert"), None),
            P(("dp", "expert"), None),
            P(("dp", "expert")),
            P(("dp", "expert"), "tensor"),
            P(("dp", "expert"), None),
            P(("dp", "expert")),
            P(("dp", "expert"), "tensor"),
            P("tensor", ("dp", "expert")),
            P(("dp", "expert")),
            P(("dp", "expert"), None),
            P(("dp", "expert"), "tensor"),
            P(("dp", "expert"), "tensor"),
            P("tensor", ("dp", "expert")),
            P("expert", "dp", "tensor"),
            P("expert", "dp", "tensor"),
            P("expert", "tensor", "dp"),
        ),
        check_vma=False,
    )
```
